32 devices in a mesh: seq: 8 (over z, core), fsdp: 4 (over y, x).
Axes of the slice: x: 2, y: 2, z: 4, core: 2. Of those that a mesh axis runs over, the one named last changes fastest.
Arguments:
- hidden_in: float32 [4, 1024, 1024], P('fsdp', 'seq'), may hold values from -6 to 6
- segment_ids: int32 [4, 1024], P('fsdp'), may hold values from 0 to 2, as said below
- norm_gain: float32 [2, 1024], replicated, may hold values from 0.5 to 1.5
- in_weight: bfloat16 [2, 1024, 4384], P(None, 'fsdp'), may hold values from -0.1875 to 0.1875
- conv_weight: float32 [2, 4, 2304], replicated, may hold values from -3 to 3
- conv_bias: float32 [2, 2304], replicated, may hold values from -3 to 3
- dt_bias: float32 [2, 32], replicated, may hold values from -8 to -3.5
- a_log: float32 [2, 32], replicated, may hold values from 0 to 1.4
- skip_weight: float32 [2, 32], replicated, may hold values from 0.5 to 1.5
- gate_norm: float32 [2, 2048], replicated, may hold values from 0.5 to 1.5
- out_weight: bfloat16 [2, 1024, 2048], P(None, 'fsdp'), may hold values from -0.125 to 0.125
- cotangent: float32 [4, 1024, 1024], P('fsdp', 'seq'), may hold values from -6 to 6
Outputs:
- hidden_out: float32 [4, 1024, 1024], P('fsdp', 'seq')
- grad_input: float32 [4, 1024, 1024], P('fsdp', 'seq')
- grad_norm_gain: float32 [2, 1024], replicated
- grad_in_weight: float32 [2, 1024, 4384], P(None, ('seq', 'fsdp'))
- grad_conv_weight: float32 [2, 4, 2304], replicated
- grad_conv_bias: float32 [2, 2304], replicated
- grad_dt_bias: float32 [2, 32], replicated
- grad_a_log: float32 [2, 32], replicated
- grad_skip: float32 [2, 32], replicated
- grad_gate_norm: float32 [2, 2048], replicated
- grad_out_weight: float32 [2, 1024, 2048], P(None, ('seq', 'fsdp'))
The draws below stay inside these ranges and needn't reach their ends.
Inputs may be any that keep to these rules, and one draw needn't show every extreme that they name: `segment_ids`: each sequence holds documents 0, 1 and 2 in order; document 1 begins within the first 128 positions and document 2 within the last 128 positions, so document 1 reaches across every piece of 128 positions.
All inputs are finite; a program needn't handle non-finite values.
Results may differ from the reference program's by a relative error of at most 0.013.
Values may be sent and summed in bfloat16 or wider, within the bound.
No kernel may reach another device: no remote copies, remote signals or barrier semaphores. Data moves between devices by JAX's collectives and lax.ppermute only.
A program may use at most 256 MiB of HBM per device.

```python
import math
from functools import partial
import jax
import jax.numpy as jnp
from jax import lax

D = 1024
INNER = 2048
HEADS = 32
HEADDIM = 64
STATE = 128
CONV = 4
LAYERS = 2
TOK_DEV = 128
XBC = 2304
PROJ = 4384
LENGTH = 1024
SEQS = 4


def draw_segment_ids(key, part):
    key = jax.random.fold_in(key, 11)
    first_key, last_key = jax.random.split(key)
    opening = jax.random.randint(first_key, (SEQS, 1), 1, TOK_DEV)
    closing = jax.random.randint(last_key, (SEQS, 1), LENGTH - TOK_DEV + 1, LENGTH)
    places = jnp.arange(LENGTH, dtype=jnp.int32)[None, :]
    return (places >= opening).astype(jnp.int32) + (places >= closing).astype(jnp.int32)


def levels(own_key, shape, shards, smallest, largest):
    level, own = 1.0, jax.random.fold_in(own_key, 6)
    for axis_at, blocks in shards:
        heights = jnp.exp(jax.random.uniform(jax.random.fold_in(own, axis_at), (blocks,), jnp.float32, smallest / len(shards), largest / len(shards)))
        level = level * jnp.repeat(heights, shape[axis_at] // blocks).reshape([-1 if axis == axis_at else 1 for axis in range(len(shape))])
    return level


def bell_draw(own_key, shape, width, bound, cuts=(), held_as=jnp.bfloat16):
    values = jax.random.normal(own_key, shape, jnp.float32) * width
    if len(cuts) > 0:
        values = levels(own_key, shape, cuts, -0.22, 0.18) * values
    return jnp.clip(values, min=-bound, max=bound).astype(held_as)


def setup_inputs(seed: int = 0) -> dict:
    keys = jax.random.split(jax.random.key(seed), 13)
    hidden_in = bell_draw(keys[0], (SEQS, LENGTH, D), 1.0, 6.0, ((0, 4), (1, 8)), jnp.float32)
    segment_ids = draw_segment_ids(jax.random.fold_in(keys[12], 71), 0)
    norm_gain = jnp.clip(1.0 + 0.1 * jax.random.normal(keys[2], (LAYERS, D), jnp.float32), 0.5, 1.5)
    in_weight = bell_draw(keys[3], (LAYERS, D, PROJ), D ** -0.5, 0.1875, ((1, 4),))
    conv_weight = bell_draw(keys[4], (LAYERS, CONV, XBC), CONV ** -0.5, 3.0, (), jnp.float32)
    conv_bias = bell_draw(keys[5], (LAYERS, XBC), 0.5, 3.0, (), jnp.float32)
    dt_bias = jnp.clip(jax.random.uniform(keys[6], (LAYERS, HEADS), jnp.float32, -8.0, -3.5), -8.0, -3.5)
    a_log = jnp.clip(jax.random.uniform(keys[7], (LAYERS, HEADS), jnp.float32, 0.0, 1.4), 0.0, 1.4)
    skip_weight = jnp.clip(jax.random.uniform(keys[8], (LAYERS, HEADS), jnp.float32, 0.5, 1.5), 0.5, 1.5)
    gate_norm = jnp.clip(1.0 + 0.1 * jax.random.normal(keys[9], (LAYERS, INNER), jnp.float32), 0.5, 1.5)
    out_weight = bell_draw(keys[10], (LAYERS, D, INNER), INNER ** -0.5, 0.125, ((1, 4),))
    cotangent = bell_draw(keys[11], (SEQS, LENGTH, D), 1.0, 6.0, ((0, 4), (1, 8)), jnp.float32)
    return dict(hidden_in=hidden_in, segment_ids=segment_ids, norm_gain=norm_gain, in_weight=in_weight, conv_weight=conv_weight, conv_bias=conv_bias, dt_bias=dt_bias, a_log=a_log, skip_weight=skip_weight, gate_norm=gate_norm, out_weight=out_weight, cotangent=cotangent)


eps = 1e-05
highest = lax.Precision.HIGHEST

@jax.custom_vjp
def low(v):
    return lax.optimization_barrier(v.astype(jnp.bfloat16)).astype(jnp.float32)

@jax.custom_vjp
def low_back(v):
    return v

def low_keep(v):
    return (low(v), None)

def low_pass(kept, grad):
    return (grad,)

def back_keep(v):
    return (v, None)

def back_low(kept, grad):
    return (low(grad),)
low.defvjp(low_keep, low_pass)
low_back.defvjp(back_keep, back_low)

def rms_scale(values, gain):
    return values * lax.rsqrt(lax.optimization_barrier(jnp.mean(values * values, axis=-1, keepdims=True)) + eps) * gain

def decays(dt_raw, dt_shift, log_rate):
    step_size = jax.nn.softplus(dt_raw + dt_shift)
    cumulative = jnp.cumsum(-jnp.exp(log_rate) * step_size, axis=0)
    return (step_size, cumulative)

def split_mixed(mixed):
    count_rows = mixed.shape[0]
    head_values = mixed[:, :INNER].reshape(count_rows, HEADS, HEADDIM)
    key_part = mixed[:, INNER:INNER + STATE]
    query_part = mixed[:, INNER + STATE:]
    return (head_values, key_part, query_part)

def block_state(mixed, dt_raw, dt_shift, log_rate, segment, segment_before):
    step_size, cumulative = decays(dt_raw, dt_shift, log_rate)
    head_values, key_part, query_part = split_mixed(mixed)
    same_end = (segment == segment[-1]).astype(mixed.dtype)
    weights_end = jnp.exp(cumulative[-1][None, :] - cumulative) * step_size * same_end[:, None]
    weighted = weights_end[:, :, None] * head_values
    local_state = jnp.einsum('thp,tn->hpn', weighted, key_part, precision=highest)
    carry_decay = jnp.exp(cumulative[-1]) * (segment[-1] == segment_before).astype(mixed.dtype)
    return (carry_decay, local_state)

def block_output(mixed, dt_raw, dt_shift, log_rate, skip_gain, state_start, segment, segment_before):
    count_rows = mixed.shape[0]
    step_size, cumulative = decays(dt_raw, dt_shift, log_rate)
    head_values, key_part, query_part = split_mixed(mixed)
    scores = jnp.dot(query_part, key_part.T, precision=highest)
    places = jnp.arange(count_rows)
    allowed = (places[:, None] >= places[None, :]) & (segment[:, None] == segment[None, :])
    spread = cumulative[:, None, :] - cumulative[None, :, :]
    pair_weight = jnp.exp(jnp.where(allowed[:, :, None], spread, -jnp.inf)) * scores[:, :, None] * step_size[None, :, :]
    within = jnp.einsum('tsh,shp->thp', pair_weight, head_values, precision=highest)
    opened = (segment == segment_before).astype(mixed.dtype)
    entering = jnp.exp(cumulative) * opened[:, None]
    reach = jnp.einsum('tn,hpn->thp', query_part, state_start, precision=highest)
    across = entering[:, :, None] * reach
    result = within + across + skip_gain[None, :, None] * head_values
    return result.reshape(count_rows, INNER)

def conv_window(extended, kernel, shift_bias, segment_ext):
    count_rows = extended.shape[0] - (CONV - 1)
    own_ids = segment_ext[CONV - 1:]
    pre_act = shift_bias[None, :] * jnp.ones((count_rows, 1), extended.dtype)
    for tap_index in range(CONV):
        same = (segment_ext[tap_index:tap_index + count_rows] == own_ids).astype(extended.dtype)
        pre_act = pre_act + kernel[tap_index][None, :] * extended[tap_index:tap_index + count_rows] * same[:, None]
    return jax.nn.silu(pre_act)

def sequence_mixer(mixed, dt_raw, dt_shift, log_rate, skip_gain, segment):
    length_now = mixed.shape[0]
    block_rows = math.gcd(length_now, 256)
    block_count = length_now // block_rows
    before_ids = jnp.concatenate([jnp.full((1,), -1, jnp.int32), segment[:-1]]).reshape(block_count, block_rows)[:, 0]

    def block_step(state_now, pieces):
        part_mixed, part_dt, part_segment, part_before = pieces
        carry_decay, local_state = block_state(part_mixed, part_dt, dt_shift, log_rate, part_segment, part_before)
        result = block_output(part_mixed, part_dt, dt_shift, log_rate, skip_gain, state_now, part_segment, part_before)
        return (carry_decay[:, None, None] * state_now + local_state, result)
    start_state = jnp.zeros((HEADS, HEADDIM, STATE), mixed.dtype)
    inputs = (mixed.reshape(block_count, block_rows, XBC), dt_raw.reshape(block_count, block_rows, HEADS), segment.reshape(block_count, block_rows), before_ids)
    _, results = lax.scan(jax.checkpoint(block_step), start_state, inputs)
    return results.reshape(length_now, INNER)

def mamba_layer(hidden, segment, gain, w_in, kernel, shift_bias, dt_shift, log_rate, skip_gain, gate_gain, w_out):
    normed = low(rms_scale(hidden, gain))
    projected = low_back(jnp.dot(normed, w_in, precision=highest))
    gate_part = projected[:, :INNER]
    raw_rows = projected[:, INNER:INNER + XBC]
    dt_raw = projected[:, INNER + XBC:]
    extended = jnp.concatenate([jnp.zeros((CONV - 1, XBC), raw_rows.dtype), raw_rows], axis=0)
    segment_ext = jnp.concatenate([jnp.full((CONV - 1,), -1, jnp.int32), segment])
    mixed = conv_window(extended, kernel, shift_bias, segment_ext)
    mixer_out = sequence_mixer(mixed, dt_raw, dt_shift, log_rate, skip_gain, segment)
    gated = low(rms_scale(mixer_out * jax.nn.silu(gate_part), gate_gain))
    return hidden + low_back(jnp.dot(gated, w_out.T, precision=highest))

def apply_layer(seq_pair, layer_params):
    return mamba_layer(seq_pair[0], seq_pair[1], *layer_params)

def reference(hidden_in, segment_ids, norm_gain, in_weight, conv_weight, conv_bias, dt_bias, a_log, skip_weight, gate_norm, out_weight, cotangent):
    params = (norm_gain, in_weight.astype(jnp.float32), conv_weight, conv_bias, dt_bias, a_log, skip_weight, gate_norm, out_weight.astype(jnp.float32))

    def forward(hidden, weights):
        for layer_index in range(LAYERS):
            layer_params = tuple((item[layer_index] for item in weights))
            one_layer = jax.checkpoint(partial(apply_layer, layer_params=layer_params))
            hidden = lax.map(one_layer, (hidden, segment_ids))
        return hidden
    result, pull_back = jax.vjp(forward, hidden_in, params)
    grad_input, grads = pull_back(cotangent)
    return (result, grad_input, grads[0], grads[1], grads[2], grads[3], grads[4], grads[5], grads[6], grads[7], grads[8])
```

```python
import functools

import jax
import jax.numpy as jnp
from jax import lax
from jax.experimental import pallas as pl
from jax.experimental.pallas import tpu as pltpu
from jax.sharding import PartitionSpec as P

D = 1024
INNER = 2048
HEADS = 32
HEADDIM = 64
STATE = 128
CONV = 4
LAYERS = 2
XBC = 2304
PROJ = 4384
LANES = 128

eps = 1e-05
low = jnp.bfloat16
full = jnp.float32
exact = lax.Precision.HIGHEST
params = pltpu.CompilerParams(vmem_limit_bytes=56 * 1024 * 1024)


def swap(block, axis, mask):
    devices = range(lax.axis_size(axis))
    return lax.ppermute(block, axis, [(k, k ^ mask) for k in devices])


def gather(block, axis):
    return [block] + [swap(block, axis, mask) for mask in range(1, lax.axis_size(axis))]


def exchange(blocks, axis):
    return [blocks[0]] + [swap(blocks[m], axis, m) for m in range(1, len(blocks))]


def gather_seq(block):
    result = [block, swap(block, "seq", 1)]
    for mask in range(2, lax.axis_size("seq"), 2):
        far = swap(block, "seq", mask)
        result += [far, swap(far, "seq", 1)]
    return result


def sum_over(values, axis):
    mask = 1
    while mask < lax.axis_size(axis):
        values = values + swap(values, axis, mask)
        mask *= 2
    return values


def dot_rows(a, b):
    return lax.dot_general(a, b, (((1,), (1,)), ((), ())), preferred_element_type=full)


def dot_tokens(a, b):
    return lax.dot_general(a, b, (((0,), (0,)), ((), ())), preferred_element_type=full)


def dot(a, b):
    return jnp.dot(a, b, preferred_element_type=full)


def iota(shape, axis):
    return lax.broadcasted_iota(jnp.int32, shape, axis)


def head_wide(columns, width):
    rows = columns.shape[0]
    left = iota((rows, LANES), 1) < HEADDIM
    return jnp.concatenate(
        [
            jnp.where(left, columns[:, 2 * p : 2 * p + 1], columns[:, 2 * p + 1 : 2 * p + 2])
            for p in range(width // LANES)
        ],
        axis=1,
    )


def head_tall(row, heads):
    return jnp.concatenate(
        [jnp.broadcast_to(row[:, h : h + 1], (HEADDIM, LANES)) for h in range(heads)], axis=0
    )


def lane_pair(values):
    left = iota(values.shape, 1) < HEADDIM
    return jnp.where(left, values, 0.0).astype(low), jnp.where(left, 0.0, values).astype(low)


def step_terms(dt_raw, head_ref, meta, rows):
    shifted = dt_raw + head_ref[0:1, :]
    step = jnp.maximum(shifted, 0.0) + jnp.log1p(jnp.exp(-jnp.abs(shifted)))
    rate = jnp.exp(head_ref[1:2, :])
    lam = -rate * step
    lower = (iota((rows, rows), 0) >= iota((rows, rows), 1)).astype(full)
    cum = jnp.dot(lower, lam, precision=exact, preferred_element_type=full)
    last = cum[rows - 1 : rows, :]
    end_decay = jnp.exp(last - cum) * meta[:, 7:8]
    entering = jnp.exp(cum) * meta[:, 6:7]
    carry = jnp.exp(last) * meta[0:1, 8:9]
    return shifted, step, rate, lam, cum, end_decay, entering, carry


def allowed_pairs(meta, segment_row, rows):
    causal = iota((rows, rows), 0) >= iota((rows, rows), 1)
    return causal & (meta[:, 9:10] == segment_row)


def assemble_rows(target, refs, part):
    for m, ref in enumerate(refs):
        rows = ref.shape[0]
        target[pl.ds(pl.multiple_of((part ^ m) * rows, rows), rows), :] = ref[...]


def forward_kernel(pieces, parts, place, *refs):
    normed = refs[:pieces]
    weights = refs[pieces : pieces + parts]
    meta_ref, segment_ref, conv_ref, head_ref, skip_ref = refs[pieces + parts : pieces + parts + 5]
    outs = refs[pieces + parts + 5 :]
    sends = outs[:pieces]
    acted_ref, normed_ref, proj_ref, pre_ref, out_ref, states_ref = outs[pieces : pieces + 6]
    state, extended, chunk_in, weight = outs[pieces + 6 :]
    chunk = pl.program_id(0)
    me, part = place[0], place[1]
    rows = chunk_in.shape[0]
    width = acted_ref.shape[1]

    @pl.when(chunk == 0)
    def _():
        assemble_rows(weight, weights, part)
        state[...] = jnp.zeros_like(state)
        extended[0:8, :] = jnp.zeros((8, extended.shape[1]), full)

    for m in range(pieces):

        @pl.when((chunk ^ me) == m)
        def _(m=m):
            chunk_in[...] = normed[m][...]

    normed_ref[...] = chunk_in[...]
    projected = dot(chunk_in[...], weight[...])
    proj_ref[...] = projected
    gate = projected[:, :width]
    raw = projected[:, width : 2 * width + 2 * STATE]
    meta = meta_ref[...]
    extended[8 : 8 + rows, :] = raw
    pre = conv_ref[4:5, :] + conv_ref[3:4, :] * raw
    for tap in range(CONV - 1):
        pre += conv_ref[tap : tap + 1, :] * (
            extended[5 + tap : 5 + tap + rows, :] * meta[:, tap : tap + 1]
        )
    extended[0:8, :] = extended[rows : rows + 8, :]
    pre_ref[...] = pre
    mixed = pre * jax.nn.sigmoid(pre)
    values = mixed[:, :width]
    keys = mixed[:, width : width + STATE].astype(low)
    queries = mixed[:, width + STATE :].astype(low)
    dt_raw = projected[:, 2 * width + 2 * STATE :]
    _, step, _, _, cum, end_decay, entering, carry = step_terms(dt_raw, head_ref, meta, rows)
    cum_t, step_t = cum.T, step.T
    scores = dot_rows(queries, keys)
    allowed = allowed_pairs(meta, segment_ref[0], rows)
    within = []
    for p in range(width // LANES):
        weights_pair = []
        for h in (2 * p, 2 * p + 1):
            spread = cum[:, h : h + 1] - cum_t[h : h + 1, :]
            decay = jnp.exp(jnp.where(allowed, spread, -1e30))
            weights_pair.append((decay * (step_t[h : h + 1, :] * scores)).astype(low))
        pair = lane_pair(values[:, LANES * p : LANES * (p + 1)])
        within.append(
            dot(jnp.concatenate(weights_pair, axis=1), jnp.concatenate(pair, axis=0))
        )
    before = state[...]
    states_ref[...] = before
    reach = dot_rows(queries, before.astype(low))
    out = (
        jnp.concatenate(within, axis=1)
        + head_wide(entering, width) * reach
        + skip_ref[...] * values
    )
    weighted = (head_wide(end_decay * step, width) * values).astype(low)
    state[...] = head_tall(carry, width // HEADDIM) * before + dot_tokens(weighted, keys)
    out_ref[...] = out
    acted = (out * (gate * jax.nn.sigmoid(gate))).astype(low)
    acted_ref[...] = acted
    for m in range(pieces):

        @pl.when((chunk ^ me) == m)
        def _(m=m):
            sends[m][...] = acted


def backward_kernel(pieces, parts, place, *refs):
    grads = refs[:pieces]
    weights = refs[pieces : pieces + parts]
    (
        meta_ref,
        segment_ref,
        conv_ref,
        head_ref,
        skip_ref,
        gain_ref,
        normed_ref,
        proj_ref,
        pre_ref,
        out_ref,
        states_ref,
    ) = refs[pieces + parts : pieces + parts + 11]
    (
        gproj_ref,
        keep_ref,
        give_ref,
        conv_out,
        head_out,
        gain_out,
        adjoint,
        extended,
        grad_in,
        weight,
        whole,
        conv_sum,
        head_sum,
    ) = refs[pieces + parts + 11 :]
    turn = pl.program_id(0)
    chunk = pieces - 1 - turn
    me, part = place[0], place[1]
    rows, width = grad_in.shape
    heads = width // HEADDIM

    @pl.when(turn == 0)
    def _():
        assemble_rows(weight, weights, part)
        adjoint[...] = jnp.zeros_like(adjoint)
        extended[rows : rows + 8, :] = jnp.zeros((8, extended.shape[1]), full)
        conv_sum[...] = jnp.zeros_like(conv_sum)
        head_sum[...] = jnp.zeros_like(head_sum)
        gain_out[...] = jnp.zeros_like(gain_out)

    for m in range(pieces):

        @pl.when((chunk ^ me) == m)
        def _(m=m):
            grad_in[...] = grads[m][...].astype(full)

    grad_acted = grad_in[...]
    meta = meta_ref[...]
    gate = proj_ref[:, :width]
    raw = proj_ref[:, width : 2 * width + 2 * STATE]
    dt_raw = proj_ref[:, 2 * width + 2 * STATE :]
    gate_open = jax.nn.sigmoid(gate)
    gate_act = gate * gate_open
    grad_out = grad_acted * gate_act
    grad_gate = grad_acted * out_ref[...] * (gate_open + gate_act * (1.0 - gate_open))
    pre = pre_ref[...]
    pre_open = jax.nn.sigmoid(pre)
    mixed = pre * pre_open
    values = mixed[:, :width]
    keys = mixed[:, width : width + STATE].astype(low)
    queries = mixed[:, width + STATE :].astype(low)
    shifted, step, rate, lam, cum, end_decay, entering, carry = step_terms(
        dt_raw, head_ref, meta, rows
    )
    cum_t, step_t = cum.T, step.T
    scores = dot_rows(queries, keys)
    allowed = allowed_pairs(meta, segment_ref[0], rows)
    before = states_ref[...]
    before_low = before.astype(low)
    after = adjoint[...]
    after_low = after.astype(low)
    from_after = dot_rows(keys, after_low)
    reach = dot_rows(queries, before_low)
    lane = iota((rows, LANES), 1)
    sub = iota((rows, LANES), 0)
    row_sums = jnp.zeros((rows, LANES), full)
    column_sums = jnp.zeros((LANES, rows), full)
    head_at = iota((LANES, rows), 0)
    grad_scores = jnp.zeros((rows, rows), full)
    grad_within = []
    for p in range(width // LANES):
        at = slice(LANES * p, LANES * (p + 1))
        value_pair = values[:, at].astype(low)
        grad_pair = lane_pair(grad_out[:, at])
        weights_pair = []
        for h, grad_head in zip((2 * p, 2 * p + 1), grad_pair):
            spread = cum[:, h : h + 1] - cum_t[h : h + 1, :]
            decay = jnp.exp(jnp.where(allowed, spread, -1e30))
            stepped = decay * step_t[h : h + 1, :]
            weights_pair.append((stepped * scores).astype(low))
            grad_weight = dot_rows(grad_head, value_pair)
            grad_scores += grad_weight * stepped
            plain = grad_weight * (decay * scores)
            row_sums += jnp.where(
                lane == h, jnp.sum(plain * step_t[h : h + 1, :], axis=1, keepdims=True), 0.0
            )
            column_sums += jnp.where(head_at == h, jnp.sum(plain, axis=0, keepdims=True), 0.0)
        grad_within.append(
            dot_tokens(jnp.concatenate(weights_pair, axis=0), jnp.concatenate(grad_pair, axis=0))
        )
    column_sums = column_sums.T
    end_step = head_wide(end_decay * step, width)
    grad_values = (
        jnp.concatenate(grad_within, axis=1) + end_step * from_after + skip_ref[...] * grad_out
    )
    grad_entering = head_wide(entering, width) * grad_out
    grad_entering_low = grad_entering.astype(low)
    grad_scores = grad_scores.astype(low)
    grad_queries = dot(grad_scores, keys) + dot(grad_entering_low, before_low)
    grad_keys = dot_tokens(grad_scores, queries) + dot((end_step * values).astype(low), after_low)
    pick = (iota((width, LANES), 0) // HEADDIM == iota((width, LANES), 1)).astype(full)
    sums = jnp.dot(
        jnp.concatenate(
            [values * from_after, grad_entering * reach, values * grad_out], axis=0
        ),
        pick,
        precision=exact,
        preferred_element_type=full,
    )
    end_sum, across_sum, skip_sum = sums[:rows], sums[rows : 2 * rows], sums[2 * rows :]
    end_part = end_decay * end_sum
    carried = jnp.sum(
        jnp.sum(after * before, axis=1, keepdims=True) * pick, axis=0, keepdims=True
    )
    grad_cum = row_sums + across_sum - step * (column_sums + end_part)
    at_last = jnp.sum(step * end_part, axis=0, keepdims=True) + carry * carried
    grad_cum += jnp.where(sub == rows - 1, at_last, 0.0)
    upper = (iota((rows, rows), 0) <= iota((rows, rows), 1)).astype(full)
    grad_lam = jnp.dot(upper, grad_cum, precision=exact, preferred_element_type=full)
    grad_step = column_sums + end_part - rate * grad_lam
    grad_dt = jnp.where(lane < heads, grad_step * jax.nn.sigmoid(shifted), 0.0)
    head_sum[0:1, :] += jnp.sum(grad_dt, axis=0, keepdims=True)
    head_sum[1:2, :] += jnp.sum(lam * grad_lam, axis=0, keepdims=True)
    head_sum[2:3, :] += jnp.sum(skip_sum, axis=0, keepdims=True)
    adjoint[...] = head_tall(carry, heads) * after + dot_tokens(grad_entering_low, queries)
    grad_pre = jnp.concatenate([grad_values, grad_keys, grad_queries], axis=1) * (
        pre_open + mixed * (1.0 - pre_open)
    )
    extended[0:rows, :] = grad_pre
    grad_raw = conv_ref[3:4, :] * grad_pre
    conv_sum[3:4, :] += jnp.sum(raw * grad_pre, axis=0, keepdims=True)
    conv_sum[4:5, :] += jnp.sum(grad_pre, axis=0, keepdims=True)
    for tap in range(CONV - 1):
        later = extended[3 - tap : 3 - tap + rows, :] * meta[:, 3 + tap : 4 + tap]
        grad_raw += conv_ref[tap : tap + 1, :] * later
        conv_sum[tap : tap + 1, :] += jnp.sum(raw * later, axis=0, keepdims=True)
    extended[rows : rows + 8, :] = extended[0:8, :]
    grad_proj = jnp.concatenate([grad_gate, grad_raw, grad_dt], axis=1).astype(low)
    gproj_ref[...] = grad_proj
    partial = dot_rows(grad_proj, weight[...])
    gain_out[0:1, :] += jnp.sum(normed_ref[...].astype(full) * partial, axis=0, keepdims=True)
    whole[...] = partial
    half = whole.shape[1] // 2
    core = me % 2
    keep_ref[...] = whole[:, pl.ds(pl.multiple_of(core * half, half), half)]
    give_ref[...] = whole[:, pl.ds(pl.multiple_of((1 - core) * half, half), half)].astype(low)

    @pl.when(turn == pieces - 1)
    def _():
        gain_out[0:1, :] = gain_out[0:1, :] / gain_ref[...]
        conv_out[...] = jnp.zeros_like(conv_out)
        conv_out[:, pl.ds(pl.multiple_of(me * width, width), width)] = conv_sum[:, :width]
        conv_out[:, INNER:] = conv_sum[:, width:]
        own = iota((LANES, LANES), 0)
        spot = (iota((LANES, LANES), 1) == own + me * heads) & (own < heads)
        head_out[...] = jnp.dot(
            head_sum[...], spot.astype(full), precision=exact, preferred_element_type=full
        )


def rows_forward_kernel(pieces, parts, place, *refs):
    acted = refs[:pieces]
    mine = refs[pieces : pieces + parts]
    other = refs[pieces + parts : pieces + 2 * parts]
    gain_ref, hidden_ref, next_ref = refs[pieces + 2 * parts : pieces + 2 * parts + 3]
    hidden_out, normed_out, rows_out, buffer, weight_mine, weight_other = refs[
        pieces + 2 * parts + 3 :
    ]
    me, part = place[0], place[1]
    core = me % 2
    assemble_rows(weight_mine, mine, part)
    assemble_rows(weight_other, other, part)
    width = acted[0].shape[1]
    for m in range(pieces):
        at = pl.multiple_of((me ^ m) * width, width)
        buffer[:, pl.ds(at, width)] = acted[m][...].astype(full)
    values = buffer[...]
    rows_out[...] = values.astype(low)
    scale = lax.rsqrt(jnp.mean(values * values, axis=1, keepdims=True) + eps)
    buffer[...] = values * scale * gain_ref[...]
    half = INNER // 2
    first = buffer[:, pl.ds(pl.multiple_of(core * half, half), half)].astype(low)
    second = buffer[:, pl.ds(pl.multiple_of((1 - core) * half, half), half)].astype(low)
    hidden = (
        hidden_ref[...] + dot_rows(first, weight_mine[...]) + dot_rows(second, weight_other[...])
    )
    hidden_out[...] = hidden
    scale = lax.rsqrt(jnp.mean(hidden * hidden, axis=1, keepdims=True) + eps)
    normed_out[...] = (hidden * scale * next_ref[...]).astype(low)


def rows_backward_kernel(pieces, parts, place, *refs):
    mine = refs[:parts]
    other = refs[parts : 2 * parts]
    gain_ref, grad_ref, rows_ref = refs[2 * parts : 2 * parts + 3]
    outs = refs[2 * parts + 3 :]
    sends = outs[:pieces]
    branch_out, gain_out, buffer, weight_mine, weight_other = outs[pieces:]
    me, part = place[0], place[1]
    core = me % 2
    assemble_rows(weight_mine, mine, part)
    assemble_rows(weight_other, other, part)
    branch = grad_ref[...].astype(low)
    half = INNER // 2
    buffer[:, pl.ds(pl.multiple_of(core * half, half), half)] = dot(branch, weight_mine[...])
    buffer[:, pl.ds(pl.multiple_of((1 - core) * half, half), half)] = dot(
        branch, weight_other[...]
    )
    grad_gated = buffer[...]
    values = rows_ref[...].astype(full)
    scale = lax.rsqrt(jnp.mean(values * values, axis=1, keepdims=True) + eps)
    unit = values * scale
    gain_out[...] = jnp.sum(grad_gated * unit, axis=0, keepdims=True)
    grad_unit = grad_gated * gain_ref[...]
    buffer[...] = scale * (
        grad_unit - unit * jnp.mean(grad_unit * unit, axis=1, keepdims=True)
    )
    branch_out[...] = (branch.astype(full) * scale).astype(low)
    width = INNER // pieces
    for m in range(pieces):
        at = pl.multiple_of((me ^ m) * width, width)
        sends[m][...] = buffer[:, pl.ds(at, width)].astype(low)


def finish_kernel(pieces, place, *refs):
    blocks = refs[:pieces]
    in_out, out_out = refs[pieces:]
    me = place[0]
    width = INNER // pieces
    heads = HEADS // pieces
    at_shared, at_dt = 2 * width, 2 * width + 2 * STATE
    shared = jnp.zeros((in_out.shape[0], 2 * STATE), full)
    own = iota((LANES, LANES), 0)
    spots = iota((LANES, LANES), 1)
    steps = jnp.zeros((in_out.shape[0], LANES), full)
    for m in range(pieces):
        block = blocks[m][...]
        where = pl.multiple_of((me ^ m) * width, width)
        in_out[:, pl.ds(where, width)] = block[:, :width].astype(full)
        in_out[:, pl.ds(INNER + where, width)] = block[:, width:at_shared].astype(full)
        out_out[:, pl.ds(where, width)] = block[:, at_dt + LANES :].astype(full)
        shared += block[:, at_shared:at_dt].astype(full)
        spot = (spots == own + (me ^ m) * heads) & (own < heads)
        steps += dot(block[:, at_dt : at_dt + LANES], spot.astype(low))
    in_out[:, 2 * INNER : INNER + XBC] = shared
    in_out[:, INNER + XBC :] = steps[:, :HEADS]


def whole_spec(array):
    return pl.BlockSpec(array.shape, lambda *_: (0,) * len(array.shape))


def run(kernel, place, grid, inputs, in_specs, outputs, out_specs, scratch, cost=None):
    out_specs = [
        whole_spec(item) if spec is None else spec for item, spec in zip(outputs, out_specs)
    ]
    in_specs = [whole_spec(item) if spec is None else spec for item, spec in zip(inputs, in_specs)]
    return pl.pallas_call(
        kernel,
        out_shape=outputs,
        grid_spec=pltpu.PrefetchScalarGridSpec(
            num_scalar_prefetch=1,
            grid=grid,
            in_specs=in_specs,
            out_specs=out_specs,
            scratch_shapes=scratch,
        ),
        compiler_params=params,
        cost_estimate=cost,
    )(place, *inputs)


def shape(*size, dtype=full):
    return jax.ShapeDtypeStruct(size, dtype)


def norm_rows(values, gain):
    scale = lax.rsqrt(jnp.mean(values * values, axis=-1, keepdims=True) + eps)
    return values * scale * gain


def per_device(
    hidden_in,
    segment_ids,
    norm_gain,
    in_weight,
    conv_weight,
    conv_bias,
    dt_bias,
    a_log,
    skip_weight,
    gate_norm,
    out_weight,
    cotangent,
):
    pieces, parts = lax.axis_size("seq"), lax.axis_size("fsdp")
    piece, part = lax.axis_index("seq"), lax.axis_index("fsdp")
    place = jnp.stack([piece, part]).astype(jnp.int32)
    tokens = hidden_in.shape[1]
    length = tokens * pieces
    heads = HEADS // pieces
    width = heads * HEADDIM
    mixed = width + 2 * STATE
    across = 2 * width + 2 * STATE + LANES
    rows_f = D // parts
    rows_out = D // (pieces * parts)
    core = piece % 2
    half = INNER // 2

    def columns(array, start, size):
        return lax.dynamic_slice_in_dim(array, start, size, array.ndim - 1)

    def own_xbc(array):
        return jnp.concatenate([columns(array, piece * width, width), array[..., INNER:]], axis=-1)

    def pad_lanes(array):
        return jnp.pad(array, [(0, 0)] * (array.ndim - 1) + [(0, LANES - array.shape[-1])])

    def own_in(layer):
        rows = in_weight[layer]
        return jnp.concatenate(
            [
                columns(rows, piece * width, width),
                columns(rows, INNER + piece * width, width),
                rows[:, 2 * INNER : INNER + XBC],
                pad_lanes(columns(rows, INNER + XBC + piece * heads, heads)),
            ],
            axis=-1,
        )

    segment = segment_ids[0]
    places = jnp.arange(length)
    flags = []
    for tap in range(CONV - 1):
        back = CONV - 1 - tap
        flags.append((segment == jnp.roll(segment, back)) & (places >= back))
    for tap in range(CONV - 1):
        back = CONV - 1 - tap
        flags.append((segment == jnp.roll(segment, -back)) & (places < length - back))
    by_piece = segment.reshape(pieces, tokens)
    before = jnp.concatenate([jnp.full((1,), -1, jnp.int32), by_piece[:-1, -1]])[:, None]
    flags.append((by_piece == before).reshape(length))
    flags.append((by_piece == by_piece[:, -1:]).reshape(length))
    flags.append(jnp.broadcast_to(by_piece[:, -1:] == before, by_piece.shape).reshape(length))
    meta = jnp.stack([flag.astype(full) for flag in flags] + [segment.astype(full)], axis=1)
    meta = jnp.pad(meta, ((0, 0), (0, 16 - meta.shape[1])))
    segment_rows = segment.astype(full).reshape(pieces, 1, tokens)

    by_chunk = lambda size, back=False: pl.BlockSpec(
        (tokens, size), (lambda i, _: (pieces - 1 - i, 0)) if back else (lambda i, _: (i, 0))
    )

    normed = norm_rows(hidden_in[0], norm_gain[0]).astype(low)
    weights_in = [gather(own_in(layer), "fsdp") for layer in range(LAYERS)]

    def both_halves(layer):
        mine = gather(columns(out_weight[layer], core * half, half), "fsdp")
        return mine, [swap(block, "seq", 1) for block in mine]

    weights_out = [both_halves(layer) for layer in range(LAYERS)]

    def layer_params(layer):
        own = lambda array: columns(array[layer], piece * heads, heads)
        conv = jnp.concatenate([conv_weight[layer], conv_bias[layer][None]], axis=0)
        conv = jnp.pad(own_xbc(conv), ((0, 3), (0, 0)))
        head = jnp.pad(pad_lanes(jnp.stack([own(dt_bias), own(a_log)])), ((0, 6), (0, 0)))
        skip = jnp.repeat(own(skip_weight), HEADDIM)[None]
        return conv, head, skip

    hidden = hidden_in[0]
    stored = []
    for layer in range(LAYERS):
        hidden_before = hidden
        conv, head, skip = layer_params(layer)
        blocks = gather_seq(normed)
        inputs = [*blocks, *weights_in[layer], meta, segment_rows, conv, head, skip]
        in_specs = [None] * len(inputs)
        in_specs[-5] = by_chunk(16)
        in_specs[-4] = pl.BlockSpec((1, 1, tokens), lambda i, _: (i, 0, 0))
        result = run(
            functools.partial(forward_kernel, pieces, parts),
            place,
            (pieces,),
            inputs,
            in_specs,
            [shape(tokens, width, dtype=low)] * pieces
            + [
                shape(length, width, dtype=low),
                shape(length, D, dtype=low),
                shape(length, across),
                shape(length, mixed),
                shape(length, width),
                shape(pieces * width, STATE),
            ],
            [None] * pieces
            + [
                by_chunk(width),
                by_chunk(D),
                by_chunk(across),
                by_chunk(mixed),
                by_chunk(width),
                pl.BlockSpec((width, STATE), lambda i, _: (i, 0)),
            ],
            [
                pltpu.VMEM((width, STATE), full),
                pltpu.VMEM((tokens + 8, mixed), full),
                pltpu.VMEM((tokens, D), low),
                pltpu.VMEM((D, across), low),
            ],
        )
        sends, (acted, normed_all, projected, pre, out, states) = result[:pieces], result[pieces:]
        received = exchange(sends, "seq")
        mine, other = weights_out[layer]
        following = norm_gain[min(layer + 1, LAYERS - 1)][None]
        inputs = [*received, *mine, *other, gate_norm[layer][None], hidden, following]
        hidden, normed, acted_rows = run(
            functools.partial(rows_forward_kernel, pieces, parts),
            place,
            (1,),
            inputs,
            [None] * len(inputs),
            [shape(tokens, D), shape(tokens, D, dtype=low), shape(tokens, INNER, dtype=low)],
            [None] * 3,
            [
                pltpu.VMEM((tokens, INNER), full),
                pltpu.VMEM((D, half), low),
                pltpu.VMEM((D, half), low),
            ],
        )
        stored.append(
            (
                hidden_before,
                (meta, segment_rows, conv, head, skip),
                (normed_all, projected, pre, out, states),
                acted,
                acted_rows,
            )
        )

    grad_hidden = cotangent[0]
    grads_weight = [None] * LAYERS
    grads_small = [None] * LAYERS
    for layer in reversed(range(LAYERS)):
        hidden_before, shared, kept, acted, acted_rows = stored[layer]
        mine, other = weights_out[layer]
        inputs = [*mine, *other, gate_norm[layer][None], grad_hidden, acted_rows]
        result = run(
            functools.partial(rows_backward_kernel, pieces, parts),
            place,
            (1,),
            inputs,
            [None] * len(inputs),
            [shape(tokens, width, dtype=low)] * pieces
            + [shape(tokens, D, dtype=low), shape(1, INNER)],
            [None] * (pieces + 2),
            [
                pltpu.VMEM((tokens, INNER), full),
                pltpu.VMEM((D, half), low),
                pltpu.VMEM((D, half), low),
            ],
        )
        sends, (branch, grad_gate_gain) = result[:pieces], result[pieces:]
        received = exchange(sends, "seq")
        branch_all = lax.all_gather(branch, "seq", axis=0, tiled=True)
        inputs = [*received, *weights_in[layer], *shared, norm_gain[layer][None], *kept]
        in_specs = [None] * len(inputs)
        in_specs[-11] = by_chunk(16, True)
        in_specs[-10] = pl.BlockSpec((1, 1, tokens), lambda i, _: (pieces - 1 - i, 0, 0))
        in_specs[-5:-1] = [by_chunk(item.shape[1], True) for item in kept[:-1]]
        in_specs[-1] = pl.BlockSpec((width, STATE), lambda i, _: (pieces - 1 - i, 0))
        grad_projected, keep, give, conv_sums, head_sums, gain_sums = run(
            functools.partial(backward_kernel, pieces, parts),
            place,
            (pieces,),
            inputs,
            in_specs,
            [
                shape(length, across, dtype=low),
                shape(length, D // 2),
                shape(length, D // 2, dtype=low),
                shape(8, XBC),
                shape(8, LANES),
                shape(8, D),
            ],
            [by_chunk(across, True), by_chunk(D // 2, True), by_chunk(D // 2, True)] + [None] * 3,
            [
                pltpu.VMEM((width, STATE), full),
                pltpu.VMEM((tokens + 8, mixed), full),
                pltpu.VMEM((tokens, width), full),
                pltpu.VMEM((D, across), low),
                pltpu.VMEM((tokens, D), full),
                pltpu.VMEM((8, mixed), full),
                pltpu.VMEM((8, LANES), full),
            ],
        )
        taken = swap(give, "seq", 1)
        chips, chip, pair = pieces // 2, piece // 2, 2 * tokens

        def paired(which):
            cut = lambda array: lax.dynamic_slice_in_dim(array, which * pair, pair, 0)
            return cut(keep) + cut(taken).astype(full)

        total = paired(chip)
        for mask in range(1, chips):
            total = total + swap(paired(chip ^ mask).astype(low), "seq", 2 * mask).astype(full)
        ours = lax.dynamic_slice_in_dim(total, core * tokens, tokens, 0)
        theirs = lax.dynamic_slice_in_dim(total, (1 - core) * tokens, tokens, 0)
        arrived = swap(theirs.astype(low), "seq", 1).astype(full)
        grad_normed = jnp.where(
            core == 0,
            jnp.concatenate([ours, arrived], axis=1),
            jnp.concatenate([arrived, ours], axis=1),
        )
        scaled = grad_normed * norm_gain[layer][None]
        scale = lax.rsqrt(jnp.mean(hidden_before * hidden_before, axis=-1, keepdims=True) + eps)
        unit = hidden_before * scale
        grad_hidden = grad_hidden + scale * (
            scaled - unit * jnp.mean(unit * scaled, axis=-1, keepdims=True)
        )
        normed_all = kept[0]
        part_in = dot_tokens(normed_all, grad_projected).astype(low)
        own_gain = columns(gate_norm[layer], piece * width, width)[None]
        part_out = (dot_tokens(branch_all, acted) * own_gain).astype(low)
        part_both = jnp.concatenate([part_in, part_out], axis=1)
        by_part = part_both.reshape(pieces, parts, rows_out, -1)

        def rows_of(which):
            cut = lax.dynamic_index_in_dim(by_part, which, 1, keepdims=False)
            return cut.reshape(pieces * rows_out, -1)

        total = rows_of(part).astype(full)
        for mask in range(1, parts):
            total = total + swap(rows_of(part ^ mask), "fsdp", mask).astype(full)
        total = total.astype(low)
        blocks = exchange(
            [
                lax.dynamic_slice_in_dim(total, (piece ^ m) * rows_out, rows_out, 0)
                for m in range(pieces)
            ],
            "seq",
        )
        grads_weight[layer] = run(
            functools.partial(finish_kernel, pieces),
            place,
            (1,),
            blocks,
            [None] * pieces,
            [shape(rows_out, PROJ), shape(rows_out, INNER)],
            [None, None],
            [],
        )
        small = jnp.concatenate(
            [conv_sums, head_sums, gain_sums, grad_gate_gain.reshape(8, -1)], axis=1
        )
        grads_small[layer] = sum_over(sum_over(small, "fsdp"), "seq")

    small = jnp.stack(grads_small)
    conv_sums, head_sums = small[:, :, :XBC], small[:, :, XBC : XBC + LANES]
    gain_sums = small[:, 0, XBC + LANES : XBC + LANES + D]
    gate_sums = small[:, :, XBC + LANES + D :].reshape(LAYERS, INNER)
    return (
        hidden[None],
        grad_hidden[None],
        gain_sums,
        jnp.stack([item[0] for item in grads_weight]),
        conv_sums[:, :CONV],
        conv_sums[:, CONV],
        head_sums[:, 0, :HEADS],
        head_sums[:, 1, :HEADS],
        head_sums[:, 2, :HEADS],
        gate_sums,
        jnp.stack([item[1] for item in grads_weight]),
    )


def solution(mesh):
    in_specs = (
        P("fsdp", "seq", None),
        P("fsdp", None),
        P(),
        P(None, "fsdp", None),
        P(),
        P(),
        P(),
        P(),
        P(),
        P(),
        P(None, "fsdp", None),
        P("fsdp", "seq", None),
    )
    out_specs = (
        P("fsdp", "seq", None),
        P("fsdp", "seq", None),
        P(),
        P(None, ("seq", "fsdp"), None),
        P(),
        P(),
        P(),
        P(),
        P(),
        P(),
        P(None, ("seq", "fsdp"), None),
    )
    return jax.shard_map(
        per_device, mesh=mesh, in_specs=in_specs, out_specs=out_specs, check_vma=False
    )
```

```python
import functools

import jax
import jax.numpy as jnp
from jax import lax
from jax.experimental import pallas as pl
from jax.experimental.pallas import tpu as pltpu
from jax.sharding import PartitionSpec as P

D = 1024
INNER = 2048
HEADS = 32
HEADDIM = 64
STATE = 128
CONV = 4
LAYERS = 2
XBC = 2304
PROJ = 4384
LANES = 128
DT_ROWS = 16

eps = 1e-05
low = jnp.bfloat16
full = jnp.float32
exact = lax.Precision.HIGHEST


def swap(block, axis, mask):
    devices = range(lax.axis_size(axis))
    return lax.ppermute(block, axis, [(k, k ^ mask) for k in devices])


def gather(block, axis):
    return [block] + [swap(block, axis, mask) for mask in range(1, lax.axis_size(axis))]


def exchange(blocks, axis):
    return [blocks[0]] + [swap(blocks[m], axis, m) for m in range(1, len(blocks))]


def gather_seq(block):
    result = [block, swap(block, "seq", 1)]
    for mask in range(2, lax.axis_size("seq"), 2):
        far = swap(block, "seq", mask)
        result += [far, swap(far, "seq", 1)]
    return result


def sum_over(values, axis):
    mask = 1
    while mask < lax.axis_size(axis):
        values = values + swap(values, axis, mask)
        mask *= 2
    return values


def after(value, *others):
    return lax.optimization_barrier((value, *others))[0]


def dot_rows(a, b):
    return lax.dot_general(a, b, (((1,), (1,)), ((), ())), preferred_element_type=full)


def dot_tokens(a, b):
    return lax.dot_general(a, b, (((0,), (0,)), ((), ())), preferred_element_type=full)


def dot(a, b):
    return jnp.dot(a, b, preferred_element_type=full)


def iota(shape, axis):
    return lax.broadcasted_iota(jnp.int32, shape, axis)


def head_wide(columns, width):
    rows = columns.shape[0]
    left = iota((rows, LANES), 1) < HEADDIM
    return jnp.concatenate(
        [
            jnp.where(left, columns[:, 2 * p : 2 * p + 1], columns[:, 2 * p + 1 : 2 * p + 2])
            for p in range(width // LANES)
        ],
        axis=1,
    )


def head_tall(row, heads):
    return jnp.concatenate(
        [jnp.broadcast_to(row[:, h : h + 1], (HEADDIM, LANES)) for h in range(heads)], axis=0
    )


def lane_pair(values):
    left = iota(values.shape, 1) < HEADDIM
    return jnp.where(left, values, 0.0).astype(low), jnp.where(left, 0.0, values).astype(low)


def step_terms(dt_raw, head_ref, meta, rows):
    shifted = dt_raw + head_ref[0:1, :]
    step = jnp.maximum(shifted, 0.0) + jnp.log1p(jnp.exp(-jnp.abs(shifted)))
    rate = jnp.exp(head_ref[1:2, :])
    lam = -rate * step
    lower = (iota((rows, rows), 0) >= iota((rows, rows), 1)).astype(full)
    cum = jnp.dot(lower, lam, precision=exact, preferred_element_type=full)
    last = cum[rows - 1 : rows, :]
    end_decay = jnp.exp(last - cum) * meta[:, 7:8]
    entering = jnp.exp(cum) * meta[:, 6:7]
    carry = jnp.exp(last) * meta[0:1, 8:9]
    return shifted, step, rate, lam, cum, end_decay, entering, carry


def allowed_pairs(meta, segment_row, rows):
    causal = iota((rows, rows), 0) >= iota((rows, rows), 1)
    return causal & (meta[:, 9:10] == segment_row)


def assemble_rows(target, refs, part):
    if len(refs) == 1:
        target[...] = refs[0][...]
        return
    for m, ref in enumerate(refs):
        rows = ref.shape[0]
        target[pl.ds(pl.multiple_of((part ^ m) * rows, rows), rows), :] = ref[...]


def assemble_columns(target, refs, part):
    rows = refs[0].shape[0] if len(refs) > 1 else target.shape[0] - LANES + DT_ROWS
    if len(refs) > 1:
        for m, ref in enumerate(refs):
            size = ref.shape[1]
            target[:rows, pl.ds(pl.multiple_of((part ^ m) * size, size), size)] = ref[...]
    else:
        size = refs[0].shape[1]
        for j in range(target.shape[1] // size):
            target[:rows, j * size : (j + 1) * size] = refs[0][j * rows : (j + 1) * rows, :]
    target[rows:, :] = jnp.zeros((target.shape[0] - rows, target.shape[1]), target.dtype)


def forward_kernel(pieces, parts, place, *refs):
    normed = refs[:pieces]
    weights = refs[pieces : pieces + parts]
    meta_ref, segment_ref, conv_ref, head_ref, skip_ref = refs[pieces + parts : pieces + parts + 5]
    outs = refs[pieces + parts + 5 :]
    sends = outs[:pieces]
    acted_ref, normed_ref, proj_ref, pre_ref, out_ref, states_ref = outs[pieces : pieces + 6]
    state, extended, chunk_in, weight = outs[pieces + 6 :]
    chunk = pl.program_id(0)
    me, part = place[0], place[1]
    rows = chunk_in.shape[0]
    width = acted_ref.shape[1]

    @pl.when(chunk == 0)
    def _():
        assemble_columns(weight, weights, part)
        state[...] = jnp.zeros_like(state)
        extended[0:8, :] = jnp.zeros((8, extended.shape[1]), full)

    for m in range(pieces):

        @pl.when((chunk ^ me) == m)
        def _(m=m):
            chunk_in[...] = normed[m][...]

    normed_ref[...] = chunk_in[...]
    projected = dot_rows(chunk_in[...], weight[...])
    proj_ref[...] = projected
    gate = projected[:, :width]
    raw = projected[:, width : 2 * width + 2 * STATE]
    meta = meta_ref[...]
    extended[8 : 8 + rows, :] = raw
    pre = conv_ref[4:5, :] + conv_ref[3:4, :] * raw
    for tap in range(CONV - 1):
        pre += conv_ref[tap : tap + 1, :] * (
            extended[5 + tap : 5 + tap + rows, :] * meta[:, tap : tap + 1]
        )
    extended[0:8, :] = extended[rows : rows + 8, :]
    pre_ref[...] = pre
    mixed = pre * jax.nn.sigmoid(pre)
    values = mixed[:, :width]
    keys = mixed[:, width : width + STATE].astype(low)
    queries = mixed[:, width + STATE :].astype(low)
    dt_raw = projected[:, 2 * width + 2 * STATE :]
    _, step, _, _, cum, end_decay, entering, carry = step_terms(dt_raw, head_ref, meta, rows)
    cum_t, step_t = cum.T, step.T
    scores = dot_rows(queries, keys)
    allowed = allowed_pairs(meta, segment_ref[0], rows)
    within = []
    for p in range(width // LANES):
        weights_pair = []
        for h in (2 * p, 2 * p + 1):
            spread = cum[:, h : h + 1] - cum_t[h : h + 1, :]
            decay = jnp.exp(jnp.where(allowed, spread, -1e30))
            weights_pair.append((decay * (step_t[h : h + 1, :] * scores)).astype(low))
        pair = lane_pair(values[:, LANES * p : LANES * (p + 1)])
        within.append(
            dot(jnp.concatenate(weights_pair, axis=1), jnp.concatenate(pair, axis=0))
        )
    before = state[...]
    states_ref[...] = before
    reach = dot_rows(queries, before.astype(low))
    out = (
        jnp.concatenate(within, axis=1)
        + head_wide(entering, width) * reach
        + skip_ref[...] * values
    )
    weighted = (head_wide(end_decay * step, width) * values).astype(low)
    state[...] = head_tall(carry, width // HEADDIM) * before + dot_tokens(weighted, keys)
    out_ref[...] = out
    acted = (out * (gate * jax.nn.sigmoid(gate))).astype(low)
    acted_ref[...] = acted
    for m in range(pieces):

        @pl.when((chunk ^ me) == m)
        def _(m=m):
            sends[m][...] = acted


def backward_kernel(pieces, parts, place, *refs):
    grads = refs[:pieces]
    weights = refs[pieces : pieces + parts]
    (
        meta_ref,
        segment_ref,
        conv_ref,
        head_ref,
        skip_ref,
        gain_ref,
        gate_gain_ref,
        normed_ref,
        proj_ref,
        pre_ref,
        out_ref,
        states_ref,
    ) = refs[pieces + parts : pieces + parts + 12]
    (
        gproj_ref,
        keep_ref,
        give_ref,
        small_ref,
        adjoint,
        extended,
        grad_in,
        weight,
        whole,
        conv_sum,
        head_sum,
        gain_sum,
    ) = refs[pieces + parts + 12 :]
    turn = pl.program_id(0)
    chunk = pieces - 1 - turn
    me, part = place[0], place[1]
    rows, width = grad_in.shape
    heads = width // HEADDIM

    @pl.when(turn == 0)
    def _():
        assemble_columns(weight, weights, part)
        adjoint[...] = jnp.zeros_like(adjoint)
        extended[rows : rows + 8, :] = jnp.zeros((8, extended.shape[1]), full)
        conv_sum[...] = jnp.zeros_like(conv_sum)
        head_sum[...] = jnp.zeros_like(head_sum)
        gain_sum[...] = jnp.zeros_like(gain_sum)

    for m in range(pieces):

        @pl.when((chunk ^ me) == m)
        def _(m=m):
            grad_in[...] = grads[m][...].astype(full)

    grad_acted = grad_in[...]
    meta = meta_ref[...]
    gate = proj_ref[:, :width]
    raw = proj_ref[:, width : 2 * width + 2 * STATE]
    dt_raw = proj_ref[:, 2 * width + 2 * STATE :]
    gate_open = jax.nn.sigmoid(gate)
    gate_act = gate * gate_open
    grad_out = grad_acted * gate_act
    grad_gate = grad_acted * out_ref[...] * (gate_open + gate_act * (1.0 - gate_open))
    pre = pre_ref[...]
    pre_open = jax.nn.sigmoid(pre)
    mixed = pre * pre_open
    values = mixed[:, :width]
    keys = mixed[:, width : width + STATE].astype(low)
    queries = mixed[:, width + STATE :].astype(low)
    shifted, step, rate, lam, cum, end_decay, entering, carry = step_terms(
        dt_raw, head_ref, meta, rows
    )
    cum_t, step_t = cum.T, step.T
    scores = dot_rows(queries, keys)
    allowed = allowed_pairs(meta, segment_ref[0], rows)
    before = states_ref[...]
    before_low = before.astype(low)
    after = adjoint[...]
    after_low = after.astype(low)
    from_after = dot_rows(keys, after_low)
    reach = dot_rows(queries, before_low)
    lane = iota((rows, LANES), 1)
    sub = iota((rows, LANES), 0)
    row_sums = jnp.zeros((rows, LANES), full)
    column_sums = jnp.zeros((LANES, rows), full)
    head_at = iota((LANES, rows), 0)
    grad_scores = jnp.zeros((rows, rows), full)
    grad_within = []
    for p in range(width // LANES):
        at = slice(LANES * p, LANES * (p + 1))
        value_pair = values[:, at].astype(low)
        grad_pair = lane_pair(grad_out[:, at])
        weights_pair = []
        for h, grad_head in zip((2 * p, 2 * p + 1), grad_pair):
            spread = cum[:, h : h + 1] - cum_t[h : h + 1, :]
            decay = jnp.exp(jnp.where(allowed, spread, -1e30))
            stepped = decay * step_t[h : h + 1, :]
            weights_pair.append((stepped * scores).astype(low))
            grad_weight = dot_rows(grad_head, value_pair)
            grad_scores += grad_weight * stepped
            plain = grad_weight * (decay * scores)
            row_sums += jnp.where(
                lane == h, jnp.sum(plain * step_t[h : h + 1, :], axis=1, keepdims=True), 0.0
            )
            column_sums += jnp.where(head_at == h, jnp.sum(plain, axis=0, keepdims=True), 0.0)
        grad_within.append(
            dot_tokens(jnp.concatenate(weights_pair, axis=0), jnp.concatenate(grad_pair, axis=0))
        )
    column_sums = column_sums.T
    end_step = head_wide(end_decay * step, width)
    grad_values = (
        jnp.concatenate(grad_within, axis=1) + end_step * from_after + skip_ref[...] * grad_out
    )
    grad_entering = head_wide(entering, width) * grad_out
    grad_entering_low = grad_entering.astype(low)
    grad_scores = grad_scores.astype(low)
    grad_queries = dot(grad_scores, keys) + dot(grad_entering_low, before_low)
    grad_keys = dot_tokens(grad_scores, queries) + dot((end_step * values).astype(low), after_low)
    pick = (iota((width, LANES), 0) // HEADDIM == iota((width, LANES), 1)).astype(full)
    sums = jnp.dot(
        jnp.concatenate(
            [values * from_after, grad_entering * reach, values * grad_out], axis=0
        ),
        pick,
        precision=exact,
        preferred_element_type=full,
    )
    end_sum, across_sum, skip_sum = sums[:rows], sums[rows : 2 * rows], sums[2 * rows :]
    end_part = end_decay * end_sum
    carried = jnp.sum(
        jnp.sum(after * before, axis=1, keepdims=True) * pick, axis=0, keepdims=True
    )
    grad_cum = row_sums + across_sum - step * (column_sums + end_part)
    at_last = jnp.sum(step * end_part, axis=0, keepdims=True) + carry * carried
    grad_cum += jnp.where(sub == rows - 1, at_last, 0.0)
    upper = (iota((rows, rows), 0) <= iota((rows, rows), 1)).astype(full)
    grad_lam = jnp.dot(upper, grad_cum, precision=exact, preferred_element_type=full)
    grad_step = column_sums + end_part - rate * grad_lam
    grad_dt = jnp.where(lane < heads, grad_step * jax.nn.sigmoid(shifted), 0.0)
    head_sum[0:1, :] += jnp.sum(grad_dt, axis=0, keepdims=True)
    head_sum[1:2, :] += jnp.sum(lam * grad_lam, axis=0, keepdims=True)
    head_sum[2:3, :] += jnp.sum(skip_sum, axis=0, keepdims=True)
    adjoint[...] = head_tall(carry, heads) * after + dot_tokens(grad_entering_low, queries)
    grad_pre = jnp.concatenate([grad_values, grad_keys, grad_queries], axis=1) * (
        pre_open + mixed * (1.0 - pre_open)
    )
    extended[0:rows, :] = grad_pre
    grad_raw = conv_ref[3:4, :] * grad_pre
    conv_sum[3:4, :] += jnp.sum(raw * grad_pre, axis=0, keepdims=True)
    conv_sum[4:5, :] += jnp.sum(grad_pre, axis=0, keepdims=True)
    for tap in range(CONV - 1):
        later = extended[3 - tap : 3 - tap + rows, :] * meta[:, 3 + tap : 4 + tap]
        grad_raw += conv_ref[tap : tap + 1, :] * later
        conv_sum[tap : tap + 1, :] += jnp.sum(raw * later, axis=0, keepdims=True)
    extended[rows : rows + 8, :] = extended[0:8, :]
    grad_proj = jnp.concatenate([grad_gate, grad_raw, grad_dt], axis=1).astype(low)
    gproj_ref[...] = grad_proj
    partial = dot(grad_proj, weight[...])
    gain_sum[...] += jnp.sum(normed_ref[...].astype(full) * partial, axis=0, keepdims=True)
    whole[...] = partial
    half = whole.shape[1] // 2
    core = me % 2
    keep_ref[...] = whole[:, pl.ds(pl.multiple_of(core * half, half), half)]
    give_ref[...] = whole[:, pl.ds(pl.multiple_of((1 - core) * half, half), half)].astype(low)

    @pl.when(turn == pieces - 1)
    def _():
        gain_sum[...] = gain_sum[...] / gain_ref[...]
        mixed_width = conv_sum.shape[1]
        small_ref[:, :mixed_width] = conv_sum[...]
        own = iota((LANES, LANES), 0)
        spot = (iota((LANES, LANES), 1) == own + me * heads) & (own < heads)
        at = mixed_width + LANES
        small_ref[:, mixed_width:at] = jnp.dot(
            head_sum[...], spot.astype(full), precision=exact, preferred_element_type=full
        )
        for ref in (gain_sum, gate_gain_ref):
            size = ref.shape[1] // 8
            for row in range(8):
                small_ref[row : row + 1, at : at + size] = ref[:, row * size : (row + 1) * size]
            at += size


def rows_forward_kernel(pieces, parts, place, *refs):
    acted = refs[:pieces]
    mine = refs[pieces : pieces + parts]
    other = refs[pieces + parts : pieces + 2 * parts]
    gain_ref, hidden_ref, next_ref = refs[pieces + 2 * parts : pieces + 2 * parts + 3]
    hidden_out, normed_out, rows_out, buffer, weight_mine, weight_other = refs[
        pieces + 2 * parts + 3 :
    ]
    me, part = place[0], place[1]
    core = me % 2
    assemble_rows(weight_mine, mine, part)
    assemble_rows(weight_other, other, part)
    width = acted[0].shape[1]
    for m in range(pieces):
        at = pl.multiple_of((me ^ m) * width, width)
        buffer[:, pl.ds(at, width)] = acted[m][...].astype(full)
    values = buffer[...]
    rows_out[...] = values.astype(low)
    scale = lax.rsqrt(jnp.mean(values * values, axis=1, keepdims=True) + eps)
    buffer[...] = values * scale * gain_ref[...]
    half = INNER // 2
    first = buffer[:, pl.ds(pl.multiple_of(core * half, half), half)].astype(low)
    second = buffer[:, pl.ds(pl.multiple_of((1 - core) * half, half), half)].astype(low)
    hidden = (
        hidden_ref[...] + dot_rows(first, weight_mine[...]) + dot_rows(second, weight_other[...])
    )
    hidden_out[...] = hidden
    scale = lax.rsqrt(jnp.mean(hidden * hidden, axis=1, keepdims=True) + eps)
    normed_out[...] = (hidden * scale * next_ref[...]).astype(low)


def rows_backward_kernel(pieces, parts, place, *refs):
    mine = refs[:parts]
    other = refs[parts : 2 * parts]
    gain_ref, grad_ref, rows_ref = refs[2 * parts : 2 * parts + 3]
    outs = refs[2 * parts + 3 :]
    sends = outs[:pieces]
    branch_out, gain_out, buffer, weight_mine, weight_other = outs[pieces:]
    me, part = place[0], place[1]
    core = me % 2
    assemble_rows(weight_mine, mine, part)
    assemble_rows(weight_other, other, part)
    branch = grad_ref[...].astype(low)
    half = INNER // 2
    buffer[:, pl.ds(pl.multiple_of(core * half, half), half)] = dot(branch, weight_mine[...])
    buffer[:, pl.ds(pl.multiple_of((1 - core) * half, half), half)] = dot(
        branch, weight_other[...]
    )
    grad_gated = buffer[...]
    values = rows_ref[...].astype(full)
    scale = lax.rsqrt(jnp.mean(values * values, axis=1, keepdims=True) + eps)
    unit = values * scale
    gain_out[...] = jnp.sum(grad_gated * unit, axis=0, keepdims=True)
    grad_unit = grad_gated * gain_ref[...]
    buffer[...] = scale * (
        grad_unit - unit * jnp.mean(grad_unit * unit, axis=1, keepdims=True)
    )
    branch_out[...] = (branch.astype(full) * scale).astype(low)
    width = INNER // pieces
    for m in range(pieces):
        at = pl.multiple_of((me ^ m) * width, width)
        sends[m][...] = buffer[:, pl.ds(at, width)].astype(low)


def pack_kernel(pieces, place, gate_ref, value_ref, shared_ref, dt_ref, out_ref):
    me = place[0]
    width = INNER // pieces
    heads = HEADS // pieces
    out_ref[:width, :] = gate_ref[0]
    out_ref[width : 2 * width, :] = value_ref[0]
    out_ref[2 * width : 2 * width + 2 * STATE, :] = shared_ref[0]
    row = iota((DT_ROWS, HEADS), 0)
    spot = (iota((DT_ROWS, HEADS), 1) == row + me * heads) & (row < heads)
    out_ref[2 * width + 2 * STATE :, :] = dot(spot.astype(low), dt_ref[0]).astype(low)


def weight_kernel(place, normed_ref, grad_ref, branch_ref, acted_ref, gain_ref, out_ref, buffer):
    across = grad_ref.shape[1]
    buffer[:, :across] = dot_tokens(normed_ref[...], grad_ref[...])
    buffer[:, across:] = dot_tokens(branch_ref[...], acted_ref[...]) * gain_ref[...]
    parts, pieces, rows, _ = out_ref.shape
    for m in range(parts):
        for j in range(pieces):
            at = (j * parts + m) * rows
            out_ref[m, j] = buffer[at : at + rows, :].astype(low)


def tree_sum(blocks):
    while len(blocks) > 1:
        blocks = [a + b for a, b in zip(blocks[::2], blocks[1::2])]
    return blocks[0]


def add_kernel(place, blocks_ref, *refs):
    out_ref = refs[-1]
    small = tree_sum([ref[...] for ref in refs[:-1]])
    first = small.astype(low)
    second = (small - first.astype(full)).astype(low)
    size = small.shape[1]
    for j in range(out_ref.shape[0]):
        out_ref[j, 0:8, :size] = first
        out_ref[j, 8:16, :size] = second
        if size < out_ref.shape[2]:
            out_ref[j, 0:16, size:] = jnp.zeros((16, out_ref.shape[2] - size), low)
        total = blocks_ref[0, j].astype(full)
        for part in range(1, blocks_ref.shape[0]):
            total += blocks_ref[part, j].astype(full)
        out_ref[j, 16:, : total.shape[1]] = total.astype(low)


def finish_kernel(pieces, place, *refs):
    stacks = refs[:LAYERS]
    (
        gain_out,
        in_out,
        kernel_out,
        bias_out,
        shift_out,
        rate_out,
        skip_out,
        gate_out,
        out_out,
    ) = refs[LAYERS:]
    width = INNER // pieces
    heads = HEADS // pieces
    at_shared, at_dt = 2 * width, 2 * width + 2 * STATE
    own = iota((LANES, LANES), 0)
    spots = iota((LANES, LANES), 1)
    for layer in range(LAYERS):
        shared = jnp.zeros((in_out.shape[1], 2 * STATE), full)
        steps = jnp.zeros((in_out.shape[1], LANES), full)
        smalls = []
        for j in range(pieces):
            block = stacks[layer][j, 16:, :]
            at = j * width
            in_out[layer, :, at : at + width] = block[:, :width].astype(full)
            in_out[layer, :, INNER + at : INNER + at + width] = block[:, width:at_shared].astype(
                full
            )
            out_out[layer, :, at : at + width] = block[
                :, at_dt + LANES : at_dt + LANES + width
            ].astype(full)
            shared += block[:, at_shared:at_dt].astype(full)
            spot = (spots == own + j * heads) & (own < heads)
            steps += dot(block[:, at_dt : at_dt + LANES], spot.astype(low))
            small = stacks[layer][j, 0:16, :].astype(full)
            small = small[0:8, :] + small[8:16, :]
            kernel_out[layer, :, at : at + width] = small[0:CONV, :width]
            bias_out[layer : layer + 1, at : at + width] = small[CONV : CONV + 1, :width]
            smalls.append(small[:, width:])
        in_out[layer, :, 2 * INNER : INNER + XBC] = shared
        in_out[layer, :, INNER + XBC :] = steps[:, :HEADS]
        total = tree_sum(smalls)
        here = slice(layer, layer + 1)
        kernel_out[layer, :, INNER:] = total[0:CONV, : 2 * STATE]
        bias_out[here, INNER:] = total[CONV : CONV + 1, : 2 * STATE]
        at = 2 * STATE
        for row, ref in enumerate((shift_out, rate_out, skip_out)):
            ref[here, :] = total[row : row + 1, at : at + HEADS]
        at += LANES
        for ref in (gain_out, gate_out):
            size = ref.shape[1] // 8
            for row in range(8):
                ref[here, row * size : (row + 1) * size] = total[row : row + 1, at : at + size]
            at += size


def whole_spec(array):
    return pl.BlockSpec(array.shape, lambda *_: (0,) * len(array.shape))


def run(kernel, place, grid, inputs, in_specs, outputs, out_specs, scratch, duration=3, limit=56):
    out_specs = [
        whole_spec(item) if spec is None else spec for item, spec in zip(outputs, out_specs)
    ]
    in_specs = [whole_spec(item) if spec is None else spec for item, spec in zip(inputs, in_specs)]
    return pl.pallas_call(
        kernel,
        out_shape=outputs,
        grid_spec=pltpu.PrefetchScalarGridSpec(
            num_scalar_prefetch=1,
            grid=grid,
            in_specs=in_specs,
            out_specs=out_specs,
            scratch_shapes=scratch,
        ),
        compiler_params=pltpu.CompilerParams(vmem_limit_bytes=limit * 1024 * 1024),
        cost_estimate=pl.CostEstimate(
            flops=duration * 10**8, bytes_accessed=duration * 3 * 10**5, transcendentals=0
        ),
    )(place, *inputs)


def shape(*size, dtype=full):
    return jax.ShapeDtypeStruct(size, dtype)


def norm_rows(values, gain):
    scale = lax.rsqrt(jnp.mean(values * values, axis=-1, keepdims=True) + eps)
    return values * scale * gain


def per_device(
    hidden_in,
    segment_ids,
    norm_gain,
    in_weight,
    conv_weight,
    conv_bias,
    dt_bias,
    a_log,
    skip_weight,
    gate_norm,
    out_weight,
    cotangent,
):
    pieces, parts = lax.axis_size("seq"), lax.axis_size("fsdp")
    piece, part = lax.axis_index("seq"), lax.axis_index("fsdp")
    place = jnp.stack([piece, part]).astype(jnp.int32)
    tokens = hidden_in.shape[1]
    length = tokens * pieces
    heads = HEADS // pieces
    width = heads * HEADDIM
    mixed = width + 2 * STATE
    across = 2 * width + 2 * STATE + LANES
    rows_f = D // parts
    rows_out = D // (pieces * parts)
    core = piece % 2
    half = INNER // 2

    def columns(array, start, size):
        return lax.dynamic_slice_in_dim(array, start, size, array.ndim - 1)

    def own_xbc(array):
        return jnp.concatenate([columns(array, piece * width, width), array[..., INNER:]], axis=-1)

    def pad_lanes(array):
        return jnp.pad(array, [(0, 0)] * (array.ndim - 1) + [(0, LANES - array.shape[-1])])

    in_turned = jnp.swapaxes(in_weight, 1, 2)

    def own_in(layer, place):
        view = lambda size, at: pl.BlockSpec((1, size, rows_f), lambda _, where: (layer, at(where), 0))
        return run(
            functools.partial(pack_kernel, pieces),
            place,
            (1,),
            [in_turned] * 4,
            [
                view(width, lambda where: where[0]),
                view(width, lambda where: where[0] + pieces),
                view(2 * STATE, lambda where: INNER // STATE),
                view(HEADS, lambda where: (INNER + XBC) // HEADS),
            ],
            [shape(2 * width + 2 * STATE + DT_ROWS, rows_f, dtype=low)],
            [None],
            [],
        )[0]

    segment = segment_ids[0]
    places = jnp.arange(length)
    flags = []
    for tap in range(CONV - 1):
        back = CONV - 1 - tap
        flags.append((segment == jnp.roll(segment, back)) & (places >= back))
    for tap in range(CONV - 1):
        back = CONV - 1 - tap
        flags.append((segment == jnp.roll(segment, -back)) & (places < length - back))
    by_piece = segment.reshape(pieces, tokens)
    before = jnp.concatenate([jnp.full((1,), -1, jnp.int32), by_piece[:-1, -1]])[:, None]
    flags.append((by_piece == before).reshape(length))
    flags.append((by_piece == by_piece[:, -1:]).reshape(length))
    flags.append(jnp.broadcast_to(by_piece[:, -1:] == before, by_piece.shape).reshape(length))
    meta = jnp.stack([flag.astype(full) for flag in flags] + [segment.astype(full)], axis=1)
    meta = jnp.pad(meta, ((0, 0), (0, 16 - meta.shape[1])))
    segment_rows = segment.astype(full).reshape(pieces, 1, tokens)

    by_chunk = lambda size, back=False: pl.BlockSpec(
        (tokens, size), (lambda i, _: (pieces - 1 - i, 0)) if back else (lambda i, _: (i, 0))
    )

    normed = norm_rows(hidden_in[0], norm_gain[0]).astype(low)
    def whole_rows(rows):
        return lax.all_gather(rows, "fsdp", axis=0, tiled=True)

    own = own_in(0, place)
    following = own_in(1, after(place, own))
    place = after(place, following)
    if rows_f % LANES == 0:
        weights_in = [gather(own, "fsdp"), [whole_rows(following)]]
    else:
        weights_in = [[lax.all_gather(item, "fsdp", axis=1, tiled=True)] for item in (own, following)]
    out_mine = [whole_rows(columns(out_weight[0], core * half, half))]
    later = after(core, *weights_in[0])
    out_mine.append(whole_rows(columns(out_weight[1], later * half, half)))
    weights_out = []

    def layer_params(layer):
        own = lambda array: columns(array[layer], piece * heads, heads)
        conv = jnp.concatenate([conv_weight[layer], conv_bias[layer][None]], axis=0)
        conv = jnp.pad(own_xbc(conv), ((0, 3), (0, 0)))
        head = jnp.pad(pad_lanes(jnp.stack([own(dt_bias), own(a_log)])), ((0, 6), (0, 0)))
        skip = jnp.repeat(own(skip_weight), HEADDIM)[None]
        return conv, head, skip

    hidden = hidden_in[0]
    stored = []
    for layer in range(LAYERS):
        hidden_before = hidden
        conv, head, skip = layer_params(layer)
        blocks = gather_seq(normed)
        inputs = [*blocks, *weights_in[layer], meta, segment_rows, conv, head, skip]
        in_specs = [None] * len(inputs)
        in_specs[-5] = by_chunk(16)
        in_specs[-4] = pl.BlockSpec((1, 1, tokens), lambda i, _: (i, 0, 0))
        result = run(
            functools.partial(forward_kernel, pieces, len(weights_in[layer])),
            place,
            (pieces,),
            inputs,
            in_specs,
            [shape(tokens, width, dtype=low)] * pieces
            + [
                shape(length, width, dtype=low),
                shape(length, D, dtype=low),
                shape(length, across),
                shape(length, mixed),
                shape(length, width),
                shape(pieces * width, STATE),
            ],
            [None] * pieces
            + [
                by_chunk(width),
                by_chunk(D),
                by_chunk(across),
                by_chunk(mixed),
                by_chunk(width),
                pl.BlockSpec((width, STATE), lambda i, _: (i, 0)),
            ],
            [
                pltpu.VMEM((width, STATE), full),
                pltpu.VMEM((tokens + 8, mixed), full),
                pltpu.VMEM((tokens, D), low),
                pltpu.VMEM((across, D), low),
            ],
            duration=16,
        )
        sends, (acted, normed_all, projected, pre, out, states) = result[:pieces], result[pieces:]
        mine = after(out_mine[layer], acted)
        weights_out.append(([mine], [swap(mine, "seq", 1)]))
        received = exchange(sends, "seq")
        mine, other = weights_out[layer]
        following = norm_gain[min(layer + 1, LAYERS - 1)][None]
        inputs = [*received, *mine, *other, gate_norm[layer][None], hidden, following]
        hidden, normed, acted_rows = run(
            functools.partial(rows_forward_kernel, pieces, len(mine)),
            place,
            (1,),
            inputs,
            [None] * len(inputs),
            [shape(tokens, D), shape(tokens, D, dtype=low), shape(tokens, INNER, dtype=low)],
            [None] * 3,
            [
                pltpu.VMEM((tokens, INNER), full),
                pltpu.VMEM((D, half), low),
                pltpu.VMEM((D, half), low),
            ],
        )
        stored.append(
            (
                hidden_before,
                (meta, segment_rows, conv, head, skip),
                (normed_all, projected, pre, out, states),
                acted,
                acted_rows,
            )
        )

    def weight_parts(layer, normed_all, grad_projected, branch_all, acted):
        own_gain = columns(gate_norm[layer], piece * width, width)[None]
        if rows_out % 16 == 0:
            return run(
                weight_kernel,
                place,
                (1,),
                [normed_all, grad_projected, branch_all, acted, own_gain],
                [None] * 5,
                [shape(parts, pieces, rows_out, across + width, dtype=low)],
                [None],
                [pltpu.VMEM((D, across + width), full)],
                duration=8,
            )[0]
        part_in = dot_tokens(normed_all, grad_projected)
        part_out = dot_tokens(branch_all, acted) * own_gain
        both = jnp.concatenate([part_in, part_out], axis=1).astype(low)
        return both.reshape(pieces, parts, rows_out, -1).swapaxes(0, 1)

    def add_parts(blocks, smalls):
        return run(
            add_kernel,
            place,
            (1,),
            [blocks, *smalls],
            [None] * (1 + parts),
            [shape(pieces, 16 + rows_out, max(across + width, smalls[0].shape[1]), dtype=low)],
            [None],
            [],
        )[0]

    def sum_pieces(partial, others):
        keep, give = partial
        taken = swap(give, "seq", 1)
        chips, chip, pair = pieces // 2, piece // 2, 2 * tokens

        def paired(which):
            cut = lambda array: lax.dynamic_slice_in_dim(array, which * pair, pair, 0)
            return cut(keep) + cut(taken).astype(full)

        total = after(paired(chip), *others)
        for mask in range(1, chips):
            total = total + swap(paired(chip ^ mask).astype(low), "seq", 2 * mask).astype(full)
        ours = lax.dynamic_slice_in_dim(total, core * tokens, tokens, 0)
        theirs = lax.dynamic_slice_in_dim(total, (1 - core) * tokens, tokens, 0)
        arrived = swap(theirs.astype(low), "seq", 1).astype(full)
        return jnp.where(
            core == 0,
            jnp.concatenate([ours, arrived], axis=1),
            jnp.concatenate([arrived, ours], axis=1),
        )

    grad_hidden = cotangent[0]
    grads_weight = [None] * LAYERS
    for layer in reversed(range(LAYERS)):
        hidden_before, shared, kept, acted, acted_rows = stored[layer]
        mine, other = weights_out[layer]
        inputs = [*mine, *other, gate_norm[layer][None], grad_hidden, acted_rows]
        result = run(
            functools.partial(rows_backward_kernel, pieces, len(mine)),
            place,
            (1,),
            inputs,
            [None] * len(inputs),
            [shape(tokens, width, dtype=low)] * pieces
            + [shape(tokens, D, dtype=low), shape(1, INNER)],
            [None] * (pieces + 2),
            [
                pltpu.VMEM((tokens, INNER), full),
                pltpu.VMEM((D, half), low),
                pltpu.VMEM((D, half), low),
            ],
        )
        sends, (branch, grad_gate_gain) = result[:pieces], result[pieces:]
        received = exchange(sends, "seq")
        if layer < LAYERS - 1:
            added = add_parts(shares, smalls)
            grads_weight[layer + 1] = lax.all_to_all(added, "seq", 0, 0, tiled=True)
            received[0] = after(received[0], added)
        branch, *received = lax.optimization_barrier((branch, *received))
        branch_all = lax.all_gather(branch, "seq", axis=0, tiled=True)
        inputs = [*received, *weights_in[layer], *shared, norm_gain[layer][None], grad_gate_gain, *kept]
        in_specs = [None] * len(inputs)
        in_specs[-12] = by_chunk(16, True)
        in_specs[-11] = pl.BlockSpec((1, 1, tokens), lambda i, _: (pieces - 1 - i, 0, 0))
        in_specs[-5:-1] = [by_chunk(item.shape[1], True) for item in kept[:-1]]
        in_specs[-1] = pl.BlockSpec((width, STATE), lambda i, _: (pieces - 1 - i, 0))
        grad_projected, *partial, small = run(
            functools.partial(backward_kernel, pieces, len(weights_in[layer])),
            place,
            (pieces,),
            inputs,
            in_specs,
            [
                shape(length, across, dtype=low),
                shape(length, D // 2),
                shape(length, D // 2, dtype=low),
                shape(8, mixed + LANES + (D + INNER) // 8),
            ],
            [
                by_chunk(across, True),
                by_chunk(D // 2, True),
                by_chunk(D // 2, True),
                None,
            ],
            [
                pltpu.VMEM((width, STATE), full),
                pltpu.VMEM((tokens + 8, mixed), full),
                pltpu.VMEM((tokens, width), full),
                pltpu.VMEM((across, D), low),
                pltpu.VMEM((tokens, D), full),
                pltpu.VMEM((8, mixed), full),
                pltpu.VMEM((8, LANES), full),
                pltpu.VMEM((1, D), full),
            ],
            duration=29,
        )
        smalls = gather(small, "fsdp")
        grad_projected = after(grad_projected, *smalls)
        weights = weight_parts(layer, kept[0], grad_projected, branch_all, acted)
        shares = lax.all_to_all(weights, "fsdp", 0, 0, tiled=True)
        if layer < LAYERS - 1:
            partial[1] = after(partial[1], weights, grads_weight[layer + 1])
        grad_normed = sum_pieces(partial, [weights])
        scaled = grad_normed * norm_gain[layer][None]
        scale = lax.rsqrt(jnp.mean(hidden_before * hidden_before, axis=-1, keepdims=True) + eps)
        unit = hidden_before * scale
        grad_hidden = grad_hidden + scale * (
            scaled - unit * jnp.mean(unit * scaled, axis=-1, keepdims=True)
        )

    added = add_parts(after(shares, grad_normed), smalls)
    grads_weight[0] = lax.all_to_all(added, "seq", 0, 0, tiled=True)
    grads = run(
        functools.partial(finish_kernel, pieces),
        place,
        (1,),
        grads_weight,
        [None] * LAYERS,
        [
            shape(LAYERS, D),
            shape(LAYERS, rows_out, PROJ),
            shape(LAYERS, CONV, XBC),
            shape(LAYERS, XBC),
            shape(LAYERS, HEADS),
            shape(LAYERS, HEADS),
            shape(LAYERS, HEADS),
            shape(LAYERS, INNER),
            shape(LAYERS, rows_out, INNER),
        ],
        [None] * 9,
        [],
    )
    return (hidden[None], grad_hidden[None], *grads)


def solution(mesh):
    in_specs = (
        P("fsdp", "seq", None),
        P("fsdp", None),
        P(),
        P(None, "fsdp", None),
        P(),
        P(),
        P(),
        P(),
        P(),
        P(),
        P(None, "fsdp", None),
        P("fsdp", "seq", None),
    )
    out_specs = (
        P("fsdp", "seq", None),
        P("fsdp", "seq", None),
        P(),
        P(None, ("seq", "fsdp"), None),
        P(),
        P(),
        P(),
        P(),
        P(),
        P(),
        P(None, ("seq", "fsdp"), None),
    )
    return jax.shard_map(
        per_device, mesh=mesh, in_specs=in_specs, out_specs=out_specs, check_vma=False
    )
```

```python
import functools

import jax
import jax.numpy as jnp
from jax import lax
from jax.experimental import pallas as pl
from jax.experimental.pallas import tpu as pltpu
from jax.sharding import PartitionSpec as P

D = 1024
INNER = 2048
HEADS = 32
HEADDIM = 64
STATE = 128
CONV = 4
LAYERS = 2
XBC = 2304
PROJ = 4384
LANES = 128
DT_ROWS = 16

eps = 1e-05
low = jnp.bfloat16
full = jnp.float32
exact = lax.Precision.HIGHEST


def swap(block, axis, mask):
    devices = range(lax.axis_size(axis))
    return lax.ppermute(block, axis, [(k, k ^ mask) for k in devices])


def gather(block, axis):
    return [block] + [swap(block, axis, mask) for mask in range(1, lax.axis_size(axis))]


def exchange(blocks, axis):
    return [blocks[0]] + [swap(blocks[m], axis, m) for m in range(1, len(blocks))]


def gather_seq(block):
    result = [block, swap(block, "seq", 1)]
    for mask in range(2, lax.axis_size("seq"), 2):
        far = swap(block, "seq", mask)
        result += [far, swap(far, "seq", 1)]
    return result


def sum_over(values, axis):
    mask = 1
    while mask < lax.axis_size(axis):
        values = values + swap(values, axis, mask)
        mask *= 2
    return values


def after(value, *others):
    return lax.optimization_barrier((value, *others))[0]


def dot_rows(a, b):
    return lax.dot_general(a, b, (((1,), (1,)), ((), ())), preferred_element_type=full)


def dot_tokens(a, b):
    return lax.dot_general(a, b, (((0,), (0,)), ((), ())), preferred_element_type=full)


def dot(a, b):
    return jnp.dot(a, b, preferred_element_type=full)


def two_terms(values):
    first = values.astype(low)
    return first, (values - first.astype(full)).astype(low)


def sum_rows(ones, values):
    both = dot(ones.astype(low), jnp.concatenate(two_terms(values), axis=1))
    size = values.shape[1]
    return both[:, :size] + both[:, size:]


def sum_lanes(values, ones):
    ones = ones.astype(low)
    return dot(jnp.concatenate(two_terms(values), axis=1), jnp.concatenate([ones, ones], axis=0))


def iota(shape, axis):
    return lax.broadcasted_iota(jnp.int32, shape, axis)


def head_wide(columns, width):
    rows = columns.shape[0]
    left = iota((rows, LANES), 1) < HEADDIM
    return jnp.concatenate(
        [
            jnp.where(left, columns[:, 2 * p : 2 * p + 1], columns[:, 2 * p + 1 : 2 * p + 2])
            for p in range(width // LANES)
        ],
        axis=1,
    )


def head_tall(row, heads):
    return jnp.concatenate(
        [jnp.broadcast_to(row[:, h : h + 1], (HEADDIM, LANES)) for h in range(heads)], axis=0
    )


def lane_pair(values):
    left = iota(values.shape, 1) < HEADDIM
    return jnp.where(left, values, 0.0).astype(low), jnp.where(left, 0.0, values).astype(low)


def step_terms(dt_raw, head_ref, meta, rows):
    shifted = dt_raw + head_ref[0:1, :]
    step = jnp.maximum(shifted, 0.0) + jnp.log1p(jnp.exp(-jnp.abs(shifted)))
    rate = jnp.exp(head_ref[1:2, :])
    lam = -rate * step
    lower = (iota((rows, rows), 0) >= iota((rows, rows), 1)).astype(full)
    cum = sum_rows(lower, lam)
    last = cum[rows - 1 : rows, :]
    end_decay = jnp.exp(last - cum) * meta[:, 7:8]
    entering = jnp.exp(cum) * meta[:, 6:7]
    carry = jnp.exp(last) * meta[0:1, 8:9]
    return shifted, step, rate, lam, cum, end_decay, entering, carry


def allowed_pairs(meta, segment_row, rows):
    causal = iota((rows, rows), 0) >= iota((rows, rows), 1)
    return causal & (meta[:, 9:10] == segment_row)


def assemble_columns(target, refs, part):
    rows = refs[0].shape[0] if len(refs) > 1 else target.shape[0] - LANES + DT_ROWS
    if len(refs) > 1:
        for m, ref in enumerate(refs):
            size = ref.shape[1]
            target[:rows, pl.ds(pl.multiple_of((part ^ m) * size, size), size)] = ref[...]
    else:
        size = refs[0].shape[1]
        for j in range(target.shape[1] // size):
            target[:rows, j * size : (j + 1) * size] = refs[0][j * rows : (j + 1) * rows, :]
    target[rows:, :] = jnp.zeros((target.shape[0] - rows, target.shape[1]), target.dtype)


def forward_kernel(pieces, parts, place, *refs):
    normed = refs[:pieces]
    weights = refs[pieces : pieces + parts]
    meta_ref, segment_ref, conv_ref, head_ref, skip_ref = refs[pieces + parts : pieces + parts + 5]
    outs = refs[pieces + parts + 5 :]
    sends = outs[:pieces]
    acted_ref, normed_ref, proj_ref, pre_ref, out_ref, states_ref = outs[pieces : pieces + 6]
    state, extended, chunk_in, weight = outs[pieces + 6 :]
    chunk = pl.program_id(0)
    me, part = place[0], place[1]
    rows = chunk_in.shape[0]
    width = acted_ref.shape[1]

    @pl.when(chunk == 0)
    def _():
        assemble_columns(weight, weights, part)
        state[...] = jnp.zeros_like(state)
        extended[0:8, :] = jnp.zeros((8, extended.shape[1]), full)

    for m in range(pieces):

        @pl.when((chunk ^ me) == m)
        def _(m=m):
            chunk_in[...] = normed[m][...]

    normed_ref[...] = chunk_in[...]
    projected = dot_rows(chunk_in[...], weight[...])
    proj_ref[...] = projected
    gate = projected[:, :width]
    raw = projected[:, width : 2 * width + 2 * STATE]
    meta = meta_ref[...]
    extended[8 : 8 + rows, :] = raw
    pre = conv_ref[4:5, :] + conv_ref[3:4, :] * raw
    for tap in range(CONV - 1):
        pre += conv_ref[tap : tap + 1, :] * (
            extended[5 + tap : 5 + tap + rows, :] * meta[:, tap : tap + 1]
        )
    extended[0:8, :] = extended[rows : rows + 8, :]
    pre_ref[...] = pre
    mixed = pre * jax.nn.sigmoid(pre)
    values = mixed[:, :width]
    keys = mixed[:, width : width + STATE].astype(low)
    queries = mixed[:, width + STATE :].astype(low)
    dt_raw = projected[:, 2 * width + 2 * STATE :]
    _, step, _, _, cum, end_decay, entering, carry = step_terms(dt_raw, head_ref, meta, rows)
    cum_t, step_t = cum.T, step.T
    scores = dot_rows(queries, keys)
    allowed = allowed_pairs(meta, segment_ref[0], rows)
    within = []
    for p in range(width // LANES):
        weights_pair = []
        for h in (2 * p, 2 * p + 1):
            spread = cum[:, h : h + 1] - cum_t[h : h + 1, :]
            decay = jnp.exp(jnp.where(allowed, spread, -1e30))
            weights_pair.append((decay * (step_t[h : h + 1, :] * scores)).astype(low))
        pair = lane_pair(values[:, LANES * p : LANES * (p + 1)])
        within.append(
            dot(jnp.concatenate(weights_pair, axis=1), jnp.concatenate(pair, axis=0))
        )
    before = state[...]
    states_ref[...] = before
    reach = dot_rows(queries, before.astype(low))
    out = (
        jnp.concatenate(within, axis=1)
        + head_wide(entering, width) * reach
        + skip_ref[...] * values
    )
    weighted = (head_wide(end_decay * step, width) * values).astype(low)
    state[...] = head_tall(carry, width // HEADDIM) * before + dot_tokens(weighted, keys)
    out_ref[...] = out
    acted = (out * (gate * jax.nn.sigmoid(gate))).astype(low)
    acted_ref[...] = acted
    for m in range(pieces):

        @pl.when((chunk ^ me) == m)
        def _(m=m):
            sends[m][...] = acted


def backward_kernel(pieces, parts, place, *refs):
    grads = refs[:pieces]
    weights = refs[pieces : pieces + parts]
    (
        meta_ref,
        segment_ref,
        conv_ref,
        head_ref,
        skip_ref,
        gain_ref,
        gate_gain_ref,
        normed_ref,
        proj_ref,
        pre_ref,
        out_ref,
        states_ref,
    ) = refs[pieces + parts : pieces + parts + 12]
    (
        gproj_ref,
        keep_ref,
        give_ref,
        small_ref,
        adjoint,
        extended,
        grad_in,
        weight,
        whole,
        conv_sum,
        head_sum,
        gain_sum,
    ) = refs[pieces + parts + 12 :]
    turn = pl.program_id(0)
    chunk = pieces - 1 - turn
    me, part = place[0], place[1]
    rows, width = grad_in.shape
    heads = width // HEADDIM

    @pl.when(turn == 0)
    def _():
        assemble_columns(weight, weights, part)
        adjoint[...] = jnp.zeros_like(adjoint)
        extended[rows : rows + 8, :] = jnp.zeros((8, extended.shape[1]), full)
        conv_sum[...] = jnp.zeros_like(conv_sum)
        head_sum[...] = jnp.zeros_like(head_sum)
        gain_sum[...] = jnp.zeros_like(gain_sum)

    for m in range(pieces):

        @pl.when((chunk ^ me) == m)
        def _(m=m):
            grad_in[...] = grads[m][...].astype(full)

    grad_acted = grad_in[...]
    meta = meta_ref[...]
    gate = proj_ref[:, :width]
    raw = proj_ref[:, width : 2 * width + 2 * STATE]
    dt_raw = proj_ref[:, 2 * width + 2 * STATE :]
    gate_open = jax.nn.sigmoid(gate)
    gate_act = gate * gate_open
    grad_out = grad_acted * gate_act
    grad_gate = grad_acted * out_ref[...] * (gate_open + gate_act * (1.0 - gate_open))
    pre = pre_ref[...]
    pre_open = jax.nn.sigmoid(pre)
    mixed = pre * pre_open
    values = mixed[:, :width]
    keys = mixed[:, width : width + STATE].astype(low)
    queries = mixed[:, width + STATE :].astype(low)
    shifted, step, rate, lam, cum, end_decay, entering, carry = step_terms(
        dt_raw, head_ref, meta, rows
    )
    cum_t, step_t = cum.T, step.T
    scores = dot_rows(queries, keys)
    allowed = allowed_pairs(meta, segment_ref[0], rows)
    before = states_ref[...]
    before_low = before.astype(low)
    after = adjoint[...]
    after_low = after.astype(low)
    from_after = dot_rows(keys, after_low)
    reach = dot_rows(queries, before_low)
    lane = iota((rows, LANES), 1)
    sub = iota((rows, LANES), 0)
    row_sums = jnp.zeros((rows, LANES), full)
    column_sums = jnp.zeros((LANES, rows), full)
    head_at = iota((LANES, rows), 0)
    grad_scores = jnp.zeros((rows, rows), full)
    grad_within = []
    for p in range(width // LANES):
        at = slice(LANES * p, LANES * (p + 1))
        value_pair = values[:, at].astype(low)
        grad_pair = lane_pair(grad_out[:, at])
        weights_pair = []
        for h, grad_head in zip((2 * p, 2 * p + 1), grad_pair):
            spread = cum[:, h : h + 1] - cum_t[h : h + 1, :]
            decay = jnp.exp(jnp.where(allowed, spread, -1e30))
            stepped = decay * step_t[h : h + 1, :]
            weights_pair.append((stepped * scores).astype(low))
            grad_weight = dot_rows(grad_head, value_pair)
            grad_scores += grad_weight * stepped
            plain = grad_weight * (decay * scores)
            row_sums += jnp.where(
                lane == h, jnp.sum(plain * step_t[h : h + 1, :], axis=1, keepdims=True), 0.0
            )
            column_sums += jnp.where(head_at == h, jnp.sum(plain, axis=0, keepdims=True), 0.0)
        grad_within.append(
            dot_tokens(jnp.concatenate(weights_pair, axis=0), jnp.concatenate(grad_pair, axis=0))
        )
    column_sums = column_sums.T
    end_step = head_wide(end_decay * step, width)
    grad_values = (
        jnp.concatenate(grad_within, axis=1) + end_step * from_after + skip_ref[...] * grad_out
    )
    grad_entering = head_wide(entering, width) * grad_out
    grad_entering_low = grad_entering.astype(low)
    grad_scores = grad_scores.astype(low)
    grad_queries = dot(grad_scores, keys) + dot(grad_entering_low, before_low)
    grad_keys = dot_tokens(grad_scores, queries) + dot((end_step * values).astype(low), after_low)
    pick = (iota((width, LANES), 0) // HEADDIM == iota((width, LANES), 1)).astype(full)
    sums = sum_lanes(
        jnp.concatenate(
            [values * from_after, grad_entering * reach, values * grad_out], axis=0
        ),
        pick,
    )
    end_sum, across_sum, skip_sum = sums[:rows], sums[rows : 2 * rows], sums[2 * rows :]
    end_part = end_decay * end_sum
    carried = jnp.sum(
        jnp.sum(after * before, axis=1, keepdims=True) * pick, axis=0, keepdims=True
    )
    grad_cum = row_sums + across_sum - step * (column_sums + end_part)
    at_last = jnp.sum(step * end_part, axis=0, keepdims=True) + carry * carried
    grad_cum += jnp.where(sub == rows - 1, at_last, 0.0)
    upper = (iota((rows, rows), 0) <= iota((rows, rows), 1)).astype(full)
    grad_lam = sum_rows(upper, grad_cum)
    grad_step = column_sums + end_part - rate * grad_lam
    grad_dt = jnp.where(lane < heads, grad_step * jax.nn.sigmoid(shifted), 0.0)
    head_sum[0:1, :] += jnp.sum(grad_dt, axis=0, keepdims=True)
    head_sum[1:2, :] += jnp.sum(lam * grad_lam, axis=0, keepdims=True)
    head_sum[2:3, :] += jnp.sum(skip_sum, axis=0, keepdims=True)
    adjoint[...] = head_tall(carry, heads) * after + dot_tokens(grad_entering_low, queries)
    grad_pre = jnp.concatenate([grad_values, grad_keys, grad_queries], axis=1) * (
        pre_open + mixed * (1.0 - pre_open)
    )
    extended[0:rows, :] = grad_pre
    grad_raw = conv_ref[3:4, :] * grad_pre
    conv_sum[3:4, :] += jnp.sum(raw * grad_pre, axis=0, keepdims=True)
    conv_sum[4:5, :] += jnp.sum(grad_pre, axis=0, keepdims=True)
    for tap in range(CONV - 1):
        later = extended[3 - tap : 3 - tap + rows, :] * meta[:, 3 + tap : 4 + tap]
        grad_raw += conv_ref[tap : tap + 1, :] * later
        conv_sum[tap : tap + 1, :] += jnp.sum(raw * later, axis=0, keepdims=True)
    extended[rows : rows + 8, :] = extended[0:8, :]
    grad_proj = jnp.concatenate([grad_gate, grad_raw, grad_dt], axis=1).astype(low)
    gproj_ref[...] = grad_proj
    partial = dot(grad_proj, weight[...])
    gain_sum[...] += jnp.sum(normed_ref[...].astype(full) * partial, axis=0, keepdims=True)
    whole[...] = partial
    half = whole.shape[1] // 2
    core = me % 2
    keep_ref[...] = whole[:, pl.ds(pl.multiple_of(core * half, half), half)]
    give_ref[...] = whole[:, pl.ds(pl.multiple_of((1 - core) * half, half), half)].astype(low)

    @pl.when(turn == pieces - 1)
    def _():
        gain_sum[...] = gain_sum[...] / gain_ref[...]
        mixed_width = conv_sum.shape[1]
        small_ref[:, :mixed_width] = conv_sum[...]
        own = iota((LANES, LANES), 0)
        spot = (iota((LANES, LANES), 1) == own + me * heads) & (own < heads)
        at = mixed_width + LANES
        small_ref[:, mixed_width:at] = jnp.dot(
            head_sum[...], spot.astype(full), precision=exact, preferred_element_type=full
        )
        for ref in (gain_sum, gate_gain_ref):
            size = ref.shape[1] // 8
            for row in range(8):
                small_ref[row : row + 1, at : at + size] = ref[:, row * size : (row + 1) * size]
            at += size


def rows_forward_kernel(pieces, parts, place, *refs):
    acted = refs[:pieces]
    mine = refs[pieces : pieces + parts]
    other = refs[pieces + parts : pieces + 2 * parts]
    gain_ref, hidden_ref, next_ref = refs[pieces + 2 * parts : pieces + 2 * parts + 3]
    hidden_out, normed_out, rows_out, buffer = refs[
        pieces + 2 * parts + 3 :
    ]
    me, part = place[0], place[1]
    core = me % 2
    weight_mine, weight_other = mine[0], other[0]
    width = acted[0].shape[1]
    for m in range(pieces):
        at = pl.multiple_of((me ^ m) * width, width)
        buffer[:, pl.ds(at, width)] = acted[m][...].astype(full)
    values = buffer[...]
    rows_out[...] = values.astype(low)
    scale = lax.rsqrt(jnp.mean(values * values, axis=1, keepdims=True) + eps)
    buffer[...] = values * scale * gain_ref[...]
    half = INNER // 2
    first = buffer[:, pl.ds(pl.multiple_of(core * half, half), half)].astype(low)
    second = buffer[:, pl.ds(pl.multiple_of((1 - core) * half, half), half)].astype(low)
    hidden = (
        hidden_ref[...] + dot_rows(first, weight_mine[...]) + dot_rows(second, weight_other[...])
    )
    hidden_out[...] = hidden
    scale = lax.rsqrt(jnp.mean(hidden * hidden, axis=1, keepdims=True) + eps)
    normed_out[...] = (hidden * scale * next_ref[...]).astype(low)


def rows_backward_kernel(pieces, parts, place, *refs):
    mine = refs[:parts]
    other = refs[parts : 2 * parts]
    gain_ref, grad_ref, rows_ref = refs[2 * parts : 2 * parts + 3]
    outs = refs[2 * parts + 3 :]
    sends = outs[:pieces]
    branch_out, gain_out, buffer = outs[pieces:]
    me, part = place[0], place[1]
    core = me % 2
    weight_mine, weight_other = mine[0], other[0]
    branch = grad_ref[...].astype(low)
    half = INNER // 2
    buffer[:, pl.ds(pl.multiple_of(core * half, half), half)] = dot(branch, weight_mine[...])
    buffer[:, pl.ds(pl.multiple_of((1 - core) * half, half), half)] = dot(
        branch, weight_other[...]
    )
    grad_gated = buffer[...]
    values = rows_ref[...].astype(full)
    scale = lax.rsqrt(jnp.mean(values * values, axis=1, keepdims=True) + eps)
    unit = values * scale
    gain_out[...] = jnp.sum(grad_gated * unit, axis=0, keepdims=True)
    grad_unit = grad_gated * gain_ref[...]
    buffer[...] = scale * (
        grad_unit - unit * jnp.mean(grad_unit * unit, axis=1, keepdims=True)
    )
    branch_out[...] = (branch.astype(full) * scale).astype(low)
    width = INNER // pieces
    for m in range(pieces):
        at = pl.multiple_of((me ^ m) * width, width)
        sends[m][...] = buffer[:, pl.ds(at, width)].astype(low)


def pack_kernel(pieces, place, gate_ref, value_ref, shared_ref, dt_ref, out_ref):
    me = place[0]
    width = INNER // pieces
    heads = HEADS // pieces
    out_ref[:width, :] = gate_ref[0]
    out_ref[width : 2 * width, :] = value_ref[0]
    out_ref[2 * width : 2 * width + 2 * STATE, :] = shared_ref[0]
    row = iota((DT_ROWS, HEADS), 0)
    spot = (iota((DT_ROWS, HEADS), 1) == row + me * heads) & (row < heads)
    out_ref[2 * width + 2 * STATE :, :] = dot(spot.astype(low), dt_ref[0]).astype(low)


def weight_kernel(place, normed_ref, grad_ref, branch_ref, acted_ref, gain_ref, out_ref, buffer):
    across = grad_ref.shape[1]
    buffer[:, :across] = dot_tokens(normed_ref[...], grad_ref[...])
    buffer[:, across:] = dot_tokens(branch_ref[...], acted_ref[...]) * gain_ref[...]
    parts, pieces, rows, _ = out_ref.shape
    for m in range(parts):
        for j in range(pieces):
            at = (j * parts + m) * rows
            out_ref[m, j] = buffer[at : at + rows, :].astype(low)


def to_owners(sends, buffer, part):
    for m, send in enumerate(sends):
        rows = send.shape[1]
        for j in range(buffer.shape[0] // (rows * len(sends))):
            at = pl.multiple_of((j * len(sends) + (part ^ m)) * rows, rows)
            send[j] = buffer[pl.ds(at, rows), :].astype(low)


def weight_in_kernel(place, normed_ref, grad_ref, *refs):
    sends, buffer = refs[:-1], refs[-1]
    buffer[...] = dot_tokens(normed_ref[...], grad_ref[...])
    to_owners(sends, buffer, place[1])


def weight_out_kernel(place, branch_ref, acted_ref, gain_ref, small_ref, *refs):
    sends, buffer = refs[:-1], refs[-1]
    buffer[...] = dot_tokens(branch_ref[...], acted_ref[...]) * gain_ref[...]
    to_owners(sends, buffer, place[1])
    width = acted_ref.shape[1]
    terms = two_terms(small_ref[...])
    for send in sends:
        for k, term in enumerate(terms):
            for b in range(term.shape[1] // width):
                send[send.shape[0] - 2 + k, 8 * b : 8 * b + 8, :] = term[
                    :, b * width : (b + 1) * width
                ]


def tree_sum(blocks):
    while len(blocks) > 1:
        blocks = [a + b for a, b in zip(blocks[::2], blocks[1::2])]
    return blocks[0]


def add_kernel(place, *refs):
    ins, out_ref = refs[:-1], refs[-1]
    pieces = out_ref.shape[0]
    if len(ins[0].shape) == 4:
        parts = ins[0].shape[0]
        columns = [[ins[0].at[k] for k in range(parts)]]
        small = tree_sum([ref[...] for ref in ins[1:]])
    else:
        parts = len(ins) // 2
        columns = [ins[:parts], ins[parts:]]
        both = tree_sum(
            [ref[pieces].astype(full) + ref[pieces + 1].astype(full) for ref in ins[parts:]]
        )
        small = jnp.concatenate([both[8 * b : 8 * b + 8] for b in range(both.shape[0] // 8)], axis=1)
    first, second = two_terms(small)
    size = small.shape[1]
    for j in range(pieces):
        out_ref[j, 0:8, :size] = first
        out_ref[j, 8:16, :size] = second
        if size < out_ref.shape[2]:
            out_ref[j, 0:16, size:] = jnp.zeros((16, out_ref.shape[2] - size), low)
        at = 0
        for blocks in columns:
            total = tree_sum([ref[j].astype(full) for ref in blocks])
            out_ref[j, 16:, at : at + total.shape[1]] = total.astype(low)
            at += total.shape[1]


def finish_kernel(pieces, place, *refs):
    stacks = refs[:LAYERS]
    (
        gain_out,
        in_out,
        kernel_out,
        bias_out,
        shift_out,
        rate_out,
        skip_out,
        gate_out,
        out_out,
    ) = refs[LAYERS:]
    width = INNER // pieces
    heads = HEADS // pieces
    at_shared, at_dt = 2 * width, 2 * width + 2 * STATE
    own = iota((LANES, LANES), 0)
    spots = iota((LANES, LANES), 1)
    for layer in range(LAYERS):
        shared = jnp.zeros((in_out.shape[1], 2 * STATE), full)
        steps = jnp.zeros((in_out.shape[1], LANES), full)
        smalls = []
        for j in range(pieces):
            block = stacks[layer][j, 16:, :]
            at = j * width
            in_out[layer, :, at : at + width] = block[:, :width].astype(full)
            in_out[layer, :, INNER + at : INNER + at + width] = block[:, width:at_shared].astype(
                full
            )
            out_out[layer, :, at : at + width] = block[
                :, at_dt + LANES : at_dt + LANES + width
            ].astype(full)
            shared += block[:, at_shared:at_dt].astype(full)
            spot = (spots == own + j * heads) & (own < heads)
            steps += dot(block[:, at_dt : at_dt + LANES], spot.astype(low))
            small = stacks[layer][j, 0:16, :].astype(full)
            small = small[0:8, :] + small[8:16, :]
            kernel_out[layer, :, at : at + width] = small[0:CONV, :width]
            bias_out[layer : layer + 1, at : at + width] = small[CONV : CONV + 1, :width]
            smalls.append(small[:, width:])
        in_out[layer, :, 2 * INNER : INNER + XBC] = shared
        in_out[layer, :, INNER + XBC :] = steps[:, :HEADS]
        total = tree_sum(smalls)
        here = slice(layer, layer + 1)
        kernel_out[layer, :, INNER:] = total[0:CONV, : 2 * STATE]
        bias_out[here, INNER:] = total[CONV : CONV + 1, : 2 * STATE]
        at = 2 * STATE
        for row, ref in enumerate((shift_out, rate_out, skip_out)):
            ref[here, :] = total[row : row + 1, at : at + HEADS]
        at += LANES
        for ref in (gain_out, gate_out):
            size = ref.shape[1] // 8
            for row in range(8):
                ref[here, row * size : (row + 1) * size] = total[row : row + 1, at : at + size]
            at += size


def whole_spec(array):
    return pl.BlockSpec(array.shape, lambda *_: (0,) * len(array.shape))


def run(kernel, place, grid, inputs, in_specs, outputs, out_specs, scratch, duration=3, limit=56):
    out_specs = [
        whole_spec(item) if spec is None else spec for item, spec in zip(outputs, out_specs)
    ]
    in_specs = [whole_spec(item) if spec is None else spec for item, spec in zip(inputs, in_specs)]
    return pl.pallas_call(
        kernel,
        out_shape=outputs,
        grid_spec=pltpu.PrefetchScalarGridSpec(
            num_scalar_prefetch=1,
            grid=grid,
            in_specs=in_specs,
            out_specs=out_specs,
            scratch_shapes=scratch,
        ),
        compiler_params=pltpu.CompilerParams(vmem_limit_bytes=limit * 1024 * 1024),
        cost_estimate=pl.CostEstimate(
            flops=duration * 10**8, bytes_accessed=duration * 3 * 10**5, transcendentals=0
        ),
    )(place, *inputs)


def shape(*size, dtype=full):
    return jax.ShapeDtypeStruct(size, dtype)


def norm_rows(values, gain):
    scale = lax.rsqrt(jnp.mean(values * values, axis=-1, keepdims=True) + eps)
    return values * scale * gain


def per_device(
    hidden_in,
    segment_ids,
    norm_gain,
    in_weight,
    conv_weight,
    conv_bias,
    dt_bias,
    a_log,
    skip_weight,
    gate_norm,
    out_weight,
    cotangent,
):
    pieces, parts = lax.axis_size("seq"), lax.axis_size("fsdp")
    piece, part = lax.axis_index("seq"), lax.axis_index("fsdp")
    place = jnp.stack([piece, part]).astype(jnp.int32)
    tokens = hidden_in.shape[1]
    length = tokens * pieces
    heads = HEADS // pieces
    width = heads * HEADDIM
    mixed = width + 2 * STATE
    across = 2 * width + 2 * STATE + LANES
    rows_f = D // parts
    rows_out = D // (pieces * parts)
    core = piece % 2
    half = INNER // 2

    def columns(array, start, size):
        return lax.dynamic_slice_in_dim(array, start, size, array.ndim - 1)

    def own_xbc(array):
        return jnp.concatenate([columns(array, piece * width, width), array[..., INNER:]], axis=-1)

    def pad_lanes(array):
        return jnp.pad(array, [(0, 0)] * (array.ndim - 1) + [(0, LANES - array.shape[-1])])

    in_turned = jnp.swapaxes(in_weight, 1, 2)

    def own_in(layer, place):
        view = lambda size, at: pl.BlockSpec((1, size, rows_f), lambda _, where: (layer, at(where), 0))
        return run(
            functools.partial(pack_kernel, pieces),
            place,
            (1,),
            [in_turned] * 4,
            [
                view(width, lambda where: where[0]),
                view(width, lambda where: where[0] + pieces),
                view(2 * STATE, lambda where: INNER // STATE),
                view(HEADS, lambda where: (INNER + XBC) // HEADS),
            ],
            [shape(2 * width + 2 * STATE + DT_ROWS, rows_f, dtype=low)],
            [None],
            [],
        )[0]

    segment = segment_ids[0]
    places = jnp.arange(length)
    flags = []
    for tap in range(CONV - 1):
        back = CONV - 1 - tap
        flags.append((segment == jnp.roll(segment, back)) & (places >= back))
    for tap in range(CONV - 1):
        back = CONV - 1 - tap
        flags.append((segment == jnp.roll(segment, -back)) & (places < length - back))
    by_piece = segment.reshape(pieces, tokens)
    before = jnp.concatenate([jnp.full((1,), -1, jnp.int32), by_piece[:-1, -1]])[:, None]
    flags.append((by_piece == before).reshape(length))
    flags.append((by_piece == by_piece[:, -1:]).reshape(length))
    flags.append(jnp.broadcast_to(by_piece[:, -1:] == before, by_piece.shape).reshape(length))
    meta = jnp.stack([flag.astype(full) for flag in flags] + [segment.astype(full)], axis=1)
    meta = jnp.pad(meta, ((0, 0), (0, 16 - meta.shape[1])))
    segment_rows = segment.astype(full).reshape(pieces, 1, tokens)

    by_chunk = lambda size, back=False: pl.BlockSpec(
        (tokens, size), (lambda i, _: (pieces - 1 - i, 0)) if back else (lambda i, _: (i, 0))
    )

    normed = norm_rows(hidden_in[0], norm_gain[0]).astype(low)
    def whole_rows(rows):
        return lax.all_gather(rows, "fsdp", axis=0, tiled=True)

    own = own_in(0, place)
    following = own_in(1, after(place, own))
    place = after(place, following)
    if rows_f % LANES == 0:
        weights_in = [gather(own, "fsdp"), [whole_rows(following)]]
    else:
        weights_in = [[lax.all_gather(item, "fsdp", axis=1, tiled=True)] for item in (own, following)]
    out_mine = [whole_rows(columns(out_weight[0], core * half, half))]
    later = after(core, *weights_in[0])
    out_mine.append(whole_rows(columns(out_weight[1], later * half, half)))
    weights_out = []

    def layer_params(layer):
        own = lambda array: columns(array[layer], piece * heads, heads)
        conv = jnp.concatenate([conv_weight[layer], conv_bias[layer][None]], axis=0)
        conv = jnp.pad(own_xbc(conv), ((0, 3), (0, 0)))
        head = jnp.pad(pad_lanes(jnp.stack([own(dt_bias), own(a_log)])), ((0, 6), (0, 0)))
        skip = jnp.repeat(own(skip_weight), HEADDIM)[None]
        return conv, head, skip

    hidden = hidden_in[0]
    stored = []
    for layer in range(LAYERS):
        hidden_before = hidden
        conv, head, skip = layer_params(layer)
        blocks = gather_seq(normed)
        inputs = [*blocks, *weights_in[layer], meta, segment_rows, conv, head, skip]
        in_specs = [None] * len(inputs)
        in_specs[-5] = by_chunk(16)
        in_specs[-4] = pl.BlockSpec((1, 1, tokens), lambda i, _: (i, 0, 0))
        result = run(
            functools.partial(forward_kernel, pieces, len(weights_in[layer])),
            place,
            (pieces,),
            inputs,
            in_specs,
            [shape(tokens, width, dtype=low)] * pieces
            + [
                shape(length, width, dtype=low),
                shape(length, D, dtype=low),
                shape(length, across),
                shape(length, mixed),
                shape(length, width),
                shape(pieces * width, STATE),
            ],
            [None] * pieces
            + [
                by_chunk(width),
                by_chunk(D),
                by_chunk(across),
                by_chunk(mixed),
                by_chunk(width),
                pl.BlockSpec((width, STATE), lambda i, _: (i, 0)),
            ],
            [
                pltpu.VMEM((width, STATE), full),
                pltpu.VMEM((tokens + 8, mixed), full),
                pltpu.VMEM((tokens, D), low),
                pltpu.VMEM((across, D), low),
            ],
            duration=16,
        )
        sends, (acted, normed_all, projected, pre, out, states) = result[:pieces], result[pieces:]
        mine = after(out_mine[layer], acted)
        weights_out.append(([mine], [swap(mine, "seq", 1)]))
        received = exchange(sends, "seq")
        mine, other = weights_out[layer]
        following = norm_gain[min(layer + 1, LAYERS - 1)][None]
        inputs = [*received, *mine, *other, gate_norm[layer][None], hidden, following]
        hidden, normed, acted_rows = run(
            functools.partial(rows_forward_kernel, pieces, len(mine)),
            place,
            (1,),
            inputs,
            [None] * len(inputs),
            [shape(tokens, D), shape(tokens, D, dtype=low), shape(tokens, INNER, dtype=low)],
            [None] * 3,
            [
                pltpu.VMEM((tokens, INNER), full),
            ],
        )
        stored.append(
            (
                hidden_before,
                (meta, segment_rows, conv, head, skip),
                (normed_all, projected, pre, out, states),
                acted,
                acted_rows,
            )
        )

    def weight_parts(layer, normed_all, grad_projected, branch_all, acted):
        own_gain = columns(gate_norm[layer], piece * width, width)[None]
        if rows_out % 16 == 0:
            return run(
                weight_kernel,
                place,
                (1,),
                [normed_all, grad_projected, branch_all, acted, own_gain],
                [None] * 5,
                [shape(parts, pieces, rows_out, across + width, dtype=low)],
                [None],
                [pltpu.VMEM((D, across + width), full)],
                duration=8,
            )[0]
        part_in = dot_tokens(normed_all, grad_projected)
        part_out = dot_tokens(branch_all, acted) * own_gain
        both = jnp.concatenate([part_in, part_out], axis=1).astype(low)
        return both.reshape(pieces, parts, rows_out, -1).swapaxes(0, 1)

    def weight_in_part(normed_all, grad_projected):
        return run(
            weight_in_kernel,
            place,
            (1,),
            [normed_all, grad_projected],
            [None] * 2,
            [shape(pieces, rows_out, across, dtype=low)] * parts,
            [None] * parts,
            [pltpu.VMEM((D, across), full)],
            duration=6,
        )

    def weight_out_part(branch_all, acted, small):
        own_gain = columns(gate_norm[0], piece * width, width)[None]
        return run(
            weight_out_kernel,
            place,
            (1,),
            [branch_all, acted, own_gain, small],
            [None] * 4,
            [shape(pieces + 2, rows_out, width, dtype=low)] * parts,
            [None] * parts,
            [pltpu.VMEM((D, width), full)],
        )

    def add_parts(blocks):
        return run(
            add_kernel,
            place,
            (1,),
            blocks,
            [None] * len(blocks),
            [shape(pieces, 16 + rows_out, block_lanes, dtype=low)],
            [None],
            [],
        )[0]

    small_lanes = mixed + LANES + (D + INNER) // 8
    block_lanes = max(across + width, small_lanes)
    apart = rows_out * width == small_lanes * 8

    def sum_pieces(partial, others):
        keep, give = partial
        taken = swap(give, "seq", 1)
        chips, chip, pair = pieces // 2, piece // 2, 2 * tokens

        def paired(which):
            cut = lambda array: lax.dynamic_slice_in_dim(array, which * pair, pair, 0)
            return cut(keep) + cut(taken).astype(full)

        total = after(paired(chip), *others)
        for mask in range(1, chips):
            total = total + swap(paired(chip ^ mask).astype(low), "seq", 2 * mask).astype(full)
        ours = lax.dynamic_slice_in_dim(total, core * tokens, tokens, 0)
        theirs = lax.dynamic_slice_in_dim(total, (1 - core) * tokens, tokens, 0)
        arrived = swap(theirs.astype(low), "seq", 1).astype(full)
        return jnp.where(
            core == 0,
            jnp.concatenate([ours, arrived], axis=1),
            jnp.concatenate([arrived, ours], axis=1),
        )

    grad_hidden = cotangent[0]
    grads_weight = [None] * LAYERS
    for layer in reversed(range(LAYERS)):
        hidden_before, shared, kept, acted, acted_rows = stored[layer]
        mine, other = weights_out[layer]
        inputs = [*mine, *other, gate_norm[layer][None], grad_hidden, acted_rows]
        result = run(
            functools.partial(rows_backward_kernel, pieces, len(mine)),
            place,
            (1,),
            inputs,
            [None] * len(inputs),
            [shape(tokens, width, dtype=low)] * pieces
            + [shape(tokens, D, dtype=low), shape(1, INNER)],
            [None] * (pieces + 2),
            [
                pltpu.VMEM((tokens, INNER), full),
            ],
        )
        sends, (branch, grad_gate_gain) = result[:pieces], result[pieces:]
        received = exchange(sends, "seq")
        if layer < LAYERS - 1:
            added = add_parts([shares, *smalls])
            grads_weight[layer + 1] = lax.all_to_all(added, "seq", 0, 0, tiled=True)
            received[0] = after(received[0], added)
        branch, *received = lax.optimization_barrier((branch, *received))
        branch_all = lax.all_gather(branch, "seq", axis=0, tiled=True)
        inputs = [*received, *weights_in[layer], *shared, norm_gain[layer][None], grad_gate_gain, *kept]
        in_specs = [None] * len(inputs)
        in_specs[-12] = by_chunk(16, True)
        in_specs[-11] = pl.BlockSpec((1, 1, tokens), lambda i, _: (pieces - 1 - i, 0, 0))
        in_specs[-5:-1] = [by_chunk(item.shape[1], True) for item in kept[:-1]]
        in_specs[-1] = pl.BlockSpec((width, STATE), lambda i, _: (pieces - 1 - i, 0))
        grad_projected, *partial, small = run(
            functools.partial(backward_kernel, pieces, len(weights_in[layer])),
            place,
            (pieces,),
            inputs,
            in_specs,
            [
                shape(length, across, dtype=low),
                shape(length, D // 2),
                shape(length, D // 2, dtype=low),
                shape(8, mixed + LANES + (D + INNER) // 8),
            ],
            [
                by_chunk(across, True),
                by_chunk(D // 2, True),
                by_chunk(D // 2, True),
                None,
            ],
            [
                pltpu.VMEM((width, STATE), full),
                pltpu.VMEM((tokens + 8, mixed), full),
                pltpu.VMEM((tokens, width), full),
                pltpu.VMEM((across, D), low),
                pltpu.VMEM((tokens, D), full),
                pltpu.VMEM((8, mixed), full),
                pltpu.VMEM((8, LANES), full),
                pltpu.VMEM((1, D), full),
            ],
            duration=29,
        )
        if layer == 0 and apart:
            weights = weight_in_part(kept[0], grad_projected)
            tails = weight_out_part(branch_all, acted, small)
            shares = exchange(weights, "fsdp")
            tails = exchange(tails, "fsdp")
            partial[1] = after(partial[1], *weights)
            grad_normed = sum_pieces(partial, tails)
        else:
            smalls = gather(small, "fsdp")
            grad_projected = after(grad_projected, *smalls)
            weights = weight_parts(layer, kept[0], grad_projected, branch_all, acted)
            shares = lax.all_to_all(weights, "fsdp", 0, 0, tiled=True)
            if layer < LAYERS - 1:
                partial[1] = after(partial[1], weights, grads_weight[layer + 1])
            grad_normed = sum_pieces(partial, [weights, *smalls])
        scaled = grad_normed * norm_gain[layer][None]
        scale = lax.rsqrt(jnp.mean(hidden_before * hidden_before, axis=-1, keepdims=True) + eps)
        unit = hidden_before * scale
        grad_hidden = grad_hidden + scale * (
            scaled - unit * jnp.mean(unit * scaled, axis=-1, keepdims=True)
        )

    blocks = [*shares, *tails] if apart else [shares, *smalls]
    blocks[0] = after(blocks[0], grad_normed, grads_weight[1])
    added = add_parts(blocks)
    grads_weight[0] = lax.all_to_all(added, "seq", 0, 0, tiled=True)
    grads = run(
        functools.partial(finish_kernel, pieces),
        place,
        (1,),
        grads_weight,
        [None] * LAYERS,
        [
            shape(LAYERS, D),
            shape(LAYERS, rows_out, PROJ),
            shape(LAYERS, CONV, XBC),
            shape(LAYERS, XBC),
            shape(LAYERS, HEADS),
            shape(LAYERS, HEADS),
            shape(LAYERS, HEADS),
            shape(LAYERS, INNER),
            shape(LAYERS, rows_out, INNER),
        ],
        [None] * 9,
        [],
    )
    return (hidden[None], grad_hidden[None], *grads)


def solution(mesh):
    in_specs = (
        P("fsdp", "seq", None),
        P("fsdp", None),
        P(),
        P(None, "fsdp", None),
        P(),
        P(),
        P(),
        P(),
        P(),
        P(),
        P(None, "fsdp", None),
        P("fsdp", "seq", None),
    )
    out_specs = (
        P("fsdp", "seq", None),
        P("fsdp", "seq", None),
        P(),
        P(None, ("seq", "fsdp"), None),
        P(),
        P(),
        P(),
        P(),
        P(),
        P(),
        P(None, ("seq", "fsdp"), None),
    )
    return jax.shard_map(
        per_device, mesh=mesh, in_specs=in_specs, out_specs=out_specs, check_vma=False
    )
```

```python
import functools

import jax
import jax.numpy as jnp
from jax import lax
from jax.experimental import pallas as pl
from jax.experimental.pallas import tpu as pltpu
from jax.sharding import PartitionSpec as P

D = 1024
INNER = 2048
HEADS = 32
HEADDIM = 64
STATE = 128
CONV = 4
LAYERS = 2
XBC = 2304
PROJ = 4384
LANES = 128
DT_ROWS = 16

eps = 1e-05
low = jnp.bfloat16
full = jnp.float32
exact = lax.Precision.HIGHEST


def swap(block, axis, mask):
    devices = range(lax.axis_size(axis))
    return lax.ppermute(block, axis, [(k, k ^ mask) for k in devices])


def gather(block, axis):
    return [block] + [swap(block, axis, mask) for mask in range(1, lax.axis_size(axis))]


def exchange(blocks, axis):
    return [blocks[0]] + [swap(blocks[m], axis, m) for m in range(1, len(blocks))]


def gather_seq(block):
    result = [block, swap(block, "seq", 1)]
    for mask in range(2, lax.axis_size("seq"), 2):
        far = swap(block, "seq", mask)
        result += [far, swap(far, "seq", 1)]
    return result


def sum_over(values, axis):
    mask = 1
    while mask < lax.axis_size(axis):
        values = values + swap(values, axis, mask)
        mask *= 2
    return values


def after(value, *others):
    return lax.optimization_barrier((value, *others))[0]


def dot_rows(a, b):
    return lax.dot_general(a, b, (((1,), (1,)), ((), ())), preferred_element_type=full)


def dot_tokens(a, b):
    return lax.dot_general(a, b, (((0,), (0,)), ((), ())), preferred_element_type=full)


def dot(a, b):
    return jnp.dot(a, b, preferred_element_type=full)


def two_terms(values):
    first = values.astype(low)
    return first, (values - first.astype(full)).astype(low)


def sum_rows(ones, values):
    both = dot(ones.astype(low), jnp.concatenate(two_terms(values), axis=1))
    size = values.shape[1]
    return both[:, :size] + both[:, size:]


def sum_lanes(values, ones):
    ones = ones.astype(low)
    return dot(jnp.concatenate(two_terms(values), axis=1), jnp.concatenate([ones, ones], axis=0))


def iota(shape, axis):
    return lax.broadcasted_iota(jnp.int32, shape, axis)


def head_wide(columns, width):
    rows = columns.shape[0]
    left = iota((rows, LANES), 1) < HEADDIM
    return jnp.concatenate(
        [
            jnp.where(left, columns[:, 2 * p : 2 * p + 1], columns[:, 2 * p + 1 : 2 * p + 2])
            for p in range(width // LANES)
        ],
        axis=1,
    )


def head_tall(row, heads):
    return jnp.concatenate(
        [jnp.broadcast_to(row[:, h : h + 1], (HEADDIM, LANES)) for h in range(heads)], axis=0
    )


def lane_pair(values):
    left = iota(values.shape, 1) < HEADDIM
    return jnp.where(left, values, 0.0).astype(low), jnp.where(left, 0.0, values).astype(low)


def step_terms(dt_raw, head_ref, meta, rows):
    shifted = dt_raw + head_ref[0:1, :]
    step = jnp.maximum(shifted, 0.0) + jnp.log1p(jnp.exp(-jnp.abs(shifted)))
    rate = jnp.exp(head_ref[1:2, :])
    lam = -rate * step
    lower = (iota((rows, rows), 0) >= iota((rows, rows), 1)).astype(full)
    cum = sum_rows(lower, lam)
    last = cum[rows - 1 : rows, :]
    end_decay = jnp.exp(last - cum) * meta[:, 7:8]
    entering = jnp.exp(cum) * meta[:, 6:7]
    carry = jnp.exp(last) * meta[0:1, 8:9]
    return shifted, step, rate, lam, cum, end_decay, entering, carry


def allowed_pairs(meta, segment_row, rows):
    causal = iota((rows, rows), 0) >= iota((rows, rows), 1)
    return causal & (meta[:, 9:10] == segment_row)


def assemble_columns(target, refs, part):
    rows = refs[0].shape[0] if len(refs) > 1 else target.shape[0] - LANES + DT_ROWS
    if len(refs) > 1:
        for m, ref in enumerate(refs):
            size = ref.shape[1]
            target[:rows, pl.ds(pl.multiple_of((part ^ m) * size, size), size)] = ref[...]
    else:
        size = refs[0].shape[1]
        for j in range(target.shape[1] // size):
            target[:rows, j * size : (j + 1) * size] = refs[0][j * rows : (j + 1) * rows, :]
    target[rows:, :] = jnp.zeros((target.shape[0] - rows, target.shape[1]), target.dtype)


def forward_kernel(pieces, parts, place, *refs):
    normed = refs[:pieces]
    weights = refs[pieces : pieces + parts]
    meta_ref, segment_ref, conv_ref, head_ref, skip_ref = refs[pieces + parts : pieces + parts + 5]
    outs = refs[pieces + parts + 5 :]
    sends = outs[:pieces]
    acted_ref, normed_ref, proj_ref, pre_ref, out_ref, states_ref = outs[pieces : pieces + 6]
    state, extended, chunk_in, weight = outs[pieces + 6 :]
    chunk = pl.program_id(0)
    me, part = place[0], place[1]
    rows = chunk_in.shape[0]
    width = acted_ref.shape[1]

    @pl.when(chunk == 0)
    def _():
        assemble_columns(weight, weights, part)
        state[...] = jnp.zeros_like(state)
        extended[0:8, :] = jnp.zeros((8, extended.shape[1]), full)

    for m in range(pieces):

        @pl.when((chunk ^ me) == m)
        def _(m=m):
            chunk_in[...] = normed[m][...]

    normed_ref[...] = chunk_in[...]
    projected = dot_rows(chunk_in[...], weight[...])
    proj_ref[...] = projected
    gate = projected[:, :width]
    raw = projected[:, width : 2 * width + 2 * STATE]
    meta = meta_ref[...]
    extended[8 : 8 + rows, :] = raw
    pre = conv_ref[4:5, :] + conv_ref[3:4, :] * raw
    for tap in range(CONV - 1):
        pre += conv_ref[tap : tap + 1, :] * (
            extended[5 + tap : 5 + tap + rows, :] * meta[:, tap : tap + 1]
        )
    extended[0:8, :] = extended[rows : rows + 8, :]
    pre_ref[...] = pre
    mixed = pre * jax.nn.sigmoid(pre)
    values = mixed[:, :width]
    keys = mixed[:, width : width + STATE].astype(low)
    queries = mixed[:, width + STATE :].astype(low)
    dt_raw = projected[:, 2 * width + 2 * STATE :]
    _, step, _, _, cum, end_decay, entering, carry = step_terms(dt_raw, head_ref, meta, rows)
    cum_t, step_t = cum.T, step.T
    scores = dot_rows(queries, keys)
    allowed = allowed_pairs(meta, segment_ref[0], rows)
    within = []
    for p in range(width // LANES):
        weights_pair = []
        for h in (2 * p, 2 * p + 1):
            spread = cum[:, h : h + 1] - cum_t[h : h + 1, :]
            decay = jnp.exp(jnp.where(allowed, spread, -1e30))
            weights_pair.append((decay * (step_t[h : h + 1, :] * scores)).astype(low))
        pair = lane_pair(values[:, LANES * p : LANES * (p + 1)])
        within.append(
            dot(jnp.concatenate(weights_pair, axis=1), jnp.concatenate(pair, axis=0))
        )
    before = state[...]
    states_ref[...] = before
    reach = dot_rows(queries, before.astype(low))
    out = (
        jnp.concatenate(within, axis=1)
        + head_wide(entering, width) * reach
        + skip_ref[...] * values
    )
    weighted = (head_wide(end_decay * step, width) * values).astype(low)
    state[...] = head_tall(carry, width // HEADDIM) * before + dot_tokens(weighted, keys)
    out_ref[...] = out
    acted = (out * (gate * jax.nn.sigmoid(gate))).astype(low)
    acted_ref[...] = acted
    for m in range(pieces):

        @pl.when((chunk ^ me) == m)
        def _(m=m):
            sends[m][...] = acted


def backward_kernel(pieces, parts, place, *refs):
    grads = refs[:pieces]
    weights = refs[pieces : pieces + parts]
    (
        meta_ref,
        segment_ref,
        conv_ref,
        head_ref,
        skip_ref,
        gain_ref,
        gate_gain_ref,
        normed_ref,
        proj_ref,
        pre_ref,
        out_ref,
        states_ref,
    ) = refs[pieces + parts : pieces + parts + 12]
    (
        gproj_ref,
        keep_ref,
        give_ref,
        small_ref,
        adjoint,
        extended,
        grad_in,
        weight,
        whole,
        conv_sum,
        head_sum,
        gain_sum,
    ) = refs[pieces + parts + 12 :]
    turn = pl.program_id(0)
    chunk = pieces - 1 - turn
    me, part = place[0], place[1]
    rows, width = grad_in.shape
    heads = width // HEADDIM

    @pl.when(turn == 0)
    def _():
        assemble_columns(weight, weights, part)
        adjoint[...] = jnp.zeros_like(adjoint)
        extended[rows : rows + 8, :] = jnp.zeros((8, extended.shape[1]), full)
        conv_sum[...] = jnp.zeros_like(conv_sum)
        head_sum[...] = jnp.zeros_like(head_sum)
        gain_sum[...] = jnp.zeros_like(gain_sum)

    for m in range(pieces):

        @pl.when((chunk ^ me) == m)
        def _(m=m):
            grad_in[...] = grads[m][...].astype(full)

    grad_acted = grad_in[...]
    meta = meta_ref[...]
    gate = proj_ref[:, :width]
    raw = proj_ref[:, width : 2 * width + 2 * STATE]
    dt_raw = proj_ref[:, 2 * width + 2 * STATE :]
    gate_open = jax.nn.sigmoid(gate)
    gate_act = gate * gate_open
    grad_out = grad_acted * gate_act
    grad_gate = grad_acted * out_ref[...] * (gate_open + gate_act * (1.0 - gate_open))
    pre = pre_ref[...]
    pre_open = jax.nn.sigmoid(pre)
    mixed = pre * pre_open
    values = mixed[:, :width]
    keys = mixed[:, width : width + STATE].astype(low)
    queries = mixed[:, width + STATE :].astype(low)
    shifted, step, rate, lam, cum, end_decay, entering, carry = step_terms(
        dt_raw, head_ref, meta, rows
    )
    cum_t, step_t = cum.T, step.T
    scores = dot_rows(queries, keys)
    allowed = allowed_pairs(meta, segment_ref[0], rows)
    before = states_ref[...]
    before_low = before.astype(low)
    after = adjoint[...]
    after_low = after.astype(low)
    from_after = dot_rows(keys, after_low)
    reach = dot_rows(queries, before_low)
    lane = iota((rows, LANES), 1)
    sub = iota((rows, LANES), 0)
    row_sums = jnp.zeros((rows, LANES), full)
    column_sums = jnp.zeros((LANES, rows), full)
    head_at = iota((LANES, rows), 0)
    grad_scores = jnp.zeros((rows, rows), full)
    grad_within = []
    for p in range(width // LANES):
        at = slice(LANES * p, LANES * (p + 1))
        value_pair = values[:, at].astype(low)
        grad_pair = lane_pair(grad_out[:, at])
        weights_pair = []
        for h, grad_head in zip((2 * p, 2 * p + 1), grad_pair):
            spread = cum[:, h : h + 1] - cum_t[h : h + 1, :]
            decay = jnp.exp(jnp.where(allowed, spread, -1e30))
            stepped = decay * step_t[h : h + 1, :]
            weights_pair.append((stepped * scores).astype(low))
            grad_weight = dot_rows(grad_head, value_pair)
            grad_scores += grad_weight * stepped
            plain = grad_weight * (decay * scores)
            row_sums += jnp.where(
                lane == h, jnp.sum(plain * step_t[h : h + 1, :], axis=1, keepdims=True), 0.0
            )
            column_sums += jnp.where(head_at == h, jnp.sum(plain, axis=0, keepdims=True), 0.0)
        grad_within.append(
            dot_tokens(jnp.concatenate(weights_pair, axis=0), jnp.concatenate(grad_pair, axis=0))
        )
    column_sums = column_sums.T
    end_step = head_wide(end_decay * step, width)
    grad_values = (
        jnp.concatenate(grad_within, axis=1) + end_step * from_after + skip_ref[...] * grad_out
    )
    grad_entering = head_wide(entering, width) * grad_out
    grad_entering_low = grad_entering.astype(low)
    grad_scores = grad_scores.astype(low)
    grad_queries = dot(grad_scores, keys) + dot(grad_entering_low, before_low)
    grad_keys = dot_tokens(grad_scores, queries) + dot((end_step * values).astype(low), after_low)
    pick = (iota((width, LANES), 0) // HEADDIM == iota((width, LANES), 1)).astype(full)
    sums = sum_lanes(
        jnp.concatenate(
            [values * from_after, grad_entering * reach, values * grad_out], axis=0
        ),
        pick,
    )
    end_sum, across_sum, skip_sum = sums[:rows], sums[rows : 2 * rows], sums[2 * rows :]
    end_part = end_decay * end_sum
    carried = jnp.sum(
        jnp.sum(after * before, axis=1, keepdims=True) * pick, axis=0, keepdims=True
    )
    grad_cum = row_sums + across_sum - step * (column_sums + end_part)
    at_last = jnp.sum(step * end_part, axis=0, keepdims=True) + carry * carried
    grad_cum += jnp.where(sub == rows - 1, at_last, 0.0)
    upper = (iota((rows, rows), 0) <= iota((rows, rows), 1)).astype(full)
    grad_lam = sum_rows(upper, grad_cum)
    grad_step = column_sums + end_part - rate * grad_lam
    grad_dt = jnp.where(lane < heads, grad_step * jax.nn.sigmoid(shifted), 0.0)
    head_sum[0:1, :] += jnp.sum(grad_dt, axis=0, keepdims=True)
    head_sum[1:2, :] += jnp.sum(lam * grad_lam, axis=0, keepdims=True)
    head_sum[2:3, :] += jnp.sum(skip_sum, axis=0, keepdims=True)
    adjoint[...] = head_tall(carry, heads) * after + dot_tokens(grad_entering_low, queries)
    grad_pre = jnp.concatenate([grad_values, grad_keys, grad_queries], axis=1) * (
        pre_open + mixed * (1.0 - pre_open)
    )
    extended[0:rows, :] = grad_pre
    grad_raw = conv_ref[3:4, :] * grad_pre
    conv_sum[3:4, :] += jnp.sum(raw * grad_pre, axis=0, keepdims=True)
    conv_sum[4:5, :] += jnp.sum(grad_pre, axis=0, keepdims=True)
    for tap in range(CONV - 1):
        later = extended[3 - tap : 3 - tap + rows, :] * meta[:, 3 + tap : 4 + tap]
        grad_raw += conv_ref[tap : tap + 1, :] * later
        conv_sum[tap : tap + 1, :] += jnp.sum(raw * later, axis=0, keepdims=True)
    extended[rows : rows + 8, :] = extended[0:8, :]
    grad_proj = jnp.concatenate([grad_gate, grad_raw, grad_dt], axis=1).astype(low)
    gproj_ref[...] = grad_proj
    partial = dot(grad_proj, weight[...])
    gain_sum[...] += jnp.sum(normed_ref[...].astype(full) * partial, axis=0, keepdims=True)
    whole[...] = partial
    half = whole.shape[1] // 2
    core = me % 2
    keep_ref[...] = whole[:, pl.ds(pl.multiple_of(core * half, half), half)]
    give_ref[...] = whole[:, pl.ds(pl.multiple_of((1 - core) * half, half), half)].astype(low)

    @pl.when(turn == pieces - 1)
    def _():
        gain_sum[...] = gain_sum[...] / gain_ref[...]
        mixed_width = conv_sum.shape[1]
        small_ref[:, :mixed_width] = conv_sum[...]
        own = iota((LANES, LANES), 0)
        spot = (iota((LANES, LANES), 1) == own + me * heads) & (own < heads)
        at = mixed_width + LANES
        small_ref[:, mixed_width:at] = jnp.dot(
            head_sum[...], spot.astype(full), precision=exact, preferred_element_type=full
        )
        for ref in (gain_sum, gate_gain_ref):
            size = ref.shape[1] // 8
            for row in range(8):
                small_ref[row : row + 1, at : at + size] = ref[:, row * size : (row + 1) * size]
            at += size


def rows_forward_kernel(pieces, parts, place, *refs):
    acted = refs[:pieces]
    mine = refs[pieces : pieces + parts]
    other = refs[pieces + parts : pieces + 2 * parts]
    gain_ref, hidden_ref, next_ref = refs[pieces + 2 * parts : pieces + 2 * parts + 3]
    hidden_out, normed_out, rows_out, buffer = refs[
        pieces + 2 * parts + 3 :
    ]
    me, part = place[0], place[1]
    core = me % 2
    weight_mine, weight_other = mine[0], other[0]
    width = acted[0].shape[1]
    for m in range(pieces):
        at = pl.multiple_of((me ^ m) * width, width)
        buffer[:, pl.ds(at, width)] = acted[m][...].astype(full)
    values = buffer[...]
    rows_out[...] = values.astype(low)
    scale = lax.rsqrt(jnp.mean(values * values, axis=1, keepdims=True) + eps)
    buffer[...] = values * scale * gain_ref[...]
    half = INNER // 2
    first = buffer[:, pl.ds(pl.multiple_of(core * half, half), half)].astype(low)
    second = buffer[:, pl.ds(pl.multiple_of((1 - core) * half, half), half)].astype(low)
    hidden = (
        hidden_ref[...] + dot_rows(first, weight_mine[...]) + dot_rows(second, weight_other[...])
    )
    hidden_out[...] = hidden
    scale = lax.rsqrt(jnp.mean(hidden * hidden, axis=1, keepdims=True) + eps)
    normed_out[...] = (hidden * scale * next_ref[...]).astype(low)


def rows_backward_kernel(pieces, parts, place, *refs):
    mine = refs[:parts]
    other = refs[parts : 2 * parts]
    gain_ref, grad_ref, rows_ref = refs[2 * parts : 2 * parts + 3]
    outs = refs[2 * parts + 3 :]
    sends = outs[:pieces]
    branch_out, gain_out, buffer = outs[pieces:]
    me, part = place[0], place[1]
    core = me % 2
    weight_mine, weight_other = mine[0], other[0]
    branch = grad_ref[...].astype(low)
    half = INNER // 2
    buffer[:, pl.ds(pl.multiple_of(core * half, half), half)] = dot(branch, weight_mine[...])
    buffer[:, pl.ds(pl.multiple_of((1 - core) * half, half), half)] = dot(
        branch, weight_other[...]
    )
    grad_gated = buffer[...]
    values = rows_ref[...].astype(full)
    scale = lax.rsqrt(jnp.mean(values * values, axis=1, keepdims=True) + eps)
    unit = values * scale
    gain_out[...] = jnp.sum(grad_gated * unit, axis=0, keepdims=True)
    grad_unit = grad_gated * gain_ref[...]
    buffer[...] = scale * (
        grad_unit - unit * jnp.mean(grad_unit * unit, axis=1, keepdims=True)
    )
    branch_out[...] = (branch.astype(full) * scale).astype(low)
    width = INNER // pieces
    for m in range(pieces):
        at = pl.multiple_of((me ^ m) * width, width)
        sends[m][...] = buffer[:, pl.ds(at, width)].astype(low)


def pack_kernel(pieces, place, gate_ref, value_ref, shared_ref, dt_ref, out_ref):
    me = place[0]
    width = INNER // pieces
    heads = HEADS // pieces
    out_ref[:width, :] = gate_ref[0]
    out_ref[width : 2 * width, :] = value_ref[0]
    out_ref[2 * width : 2 * width + 2 * STATE, :] = shared_ref[0]
    row = iota((DT_ROWS, HEADS), 0)
    spot = (iota((DT_ROWS, HEADS), 1) == row + me * heads) & (row < heads)
    out_ref[2 * width + 2 * STATE :, :] = dot(spot.astype(low), dt_ref[0]).astype(low)


def weight_kernel(place, normed_ref, grad_ref, branch_ref, acted_ref, gain_ref, out_ref, buffer):
    across = grad_ref.shape[1]
    buffer[:, :across] = dot_tokens(normed_ref[...], grad_ref[...])
    buffer[:, across:] = dot_tokens(branch_ref[...], acted_ref[...]) * gain_ref[...]
    parts, pieces, rows, _ = out_ref.shape
    for m in range(parts):
        for j in range(pieces):
            at = (j * parts + m) * rows
            out_ref[m, j] = buffer[at : at + rows, :].astype(low)


def rows_top_kernel(pieces, parts, place, *refs):
    ins = pieces + 2 * parts + 3
    weights = refs[pieces : pieces + 2 * parts]
    gain_ref, grad_ref = refs[ins - 3], refs[ins]
    hidden_out, normed_out, rows_out = refs[ins + 1 : ins + 4]
    outs, buffer = refs[ins + 4 : -1], refs[-1]
    rows_forward_kernel(
        pieces, parts, place, *refs[:ins], hidden_out, normed_out, rows_out, buffer
    )
    rows_backward_kernel(
        pieces, parts, place, *weights, gain_ref, grad_ref, rows_out, *outs, buffer
    )


def to_owners(sends, buffer, part):
    for m, send in enumerate(sends):
        rows = send.shape[1]
        for j in range(buffer.shape[0] // (rows * len(sends))):
            at = pl.multiple_of((j * len(sends) + (part ^ m)) * rows, rows)
            send[j] = buffer[pl.ds(at, rows), :].astype(low)


def weight_in_kernel(place, normed_ref, grad_ref, *refs):
    sends, buffer = refs[:-1], refs[-1]
    buffer[...] = dot_tokens(normed_ref[...], grad_ref[...])
    to_owners(sends, buffer, place[1])


def weight_out_kernel(place, branch_ref, acted_ref, gain_ref, small_ref, *refs):
    sends, buffer = refs[:-1], refs[-1]
    buffer[...] = dot_tokens(branch_ref[...], acted_ref[...]) * gain_ref[...]
    to_owners(sends, buffer, place[1])
    width = acted_ref.shape[1]
    terms = two_terms(small_ref[...])
    for send in sends:
        for k, term in enumerate(terms):
            for b in range(term.shape[1] // width):
                send[send.shape[0] - 2 + k, 8 * b : 8 * b + 8, :] = term[
                    :, b * width : (b + 1) * width
                ]


def tree_sum(blocks):
    while len(blocks) > 1:
        blocks = [a + b for a, b in zip(blocks[::2], blocks[1::2])]
    return blocks[0]


def add_kernel(place, *refs):
    ins, out_ref = refs[:-1], refs[-1]
    pieces = out_ref.shape[0]
    if len(ins[0].shape) == 4:
        parts = ins[0].shape[0]
        columns = [[ins[0].at[k] for k in range(parts)]]
        small = tree_sum([ref[...] for ref in ins[1:]])
    else:
        parts = len(ins) // 2
        columns = [ins[:parts], ins[parts:]]
        both = tree_sum(
            [ref[pieces].astype(full) + ref[pieces + 1].astype(full) for ref in ins[parts:]]
        )
        small = jnp.concatenate([both[8 * b : 8 * b + 8] for b in range(both.shape[0] // 8)], axis=1)
    first, second = two_terms(small)
    size = small.shape[1]
    for j in range(pieces):
        out_ref[j, 0:8, :size] = first
        out_ref[j, 8:16, :size] = second
        if size < out_ref.shape[2]:
            out_ref[j, 0:16, size:] = jnp.zeros((16, out_ref.shape[2] - size), low)
        at = 0
        for blocks in columns:
            total = tree_sum([ref[j].astype(full) for ref in blocks])
            out_ref[j, 16:, at : at + total.shape[1]] = total.astype(low)
            at += total.shape[1]


def finish_kernel(pieces, place, *refs):
    stacks = refs[:LAYERS]
    (
        gain_out,
        in_out,
        kernel_out,
        bias_out,
        shift_out,
        rate_out,
        skip_out,
        gate_out,
        out_out,
    ) = refs[LAYERS:]
    width = INNER // pieces
    heads = HEADS // pieces
    at_shared, at_dt = 2 * width, 2 * width + 2 * STATE
    own = iota((LANES, LANES), 0)
    spots = iota((LANES, LANES), 1)
    for layer in range(LAYERS):
        shared = jnp.zeros((in_out.shape[1], 2 * STATE), full)
        steps = jnp.zeros((in_out.shape[1], LANES), full)
        smalls = []
        for j in range(pieces):
            block = stacks[layer][j, 16:, :]
            at = j * width
            in_out[layer, :, at : at + width] = block[:, :width].astype(full)
            in_out[layer, :, INNER + at : INNER + at + width] = block[:, width:at_shared].astype(
                full
            )
            out_out[layer, :, at : at + width] = block[
                :, at_dt + LANES : at_dt + LANES + width
            ].astype(full)
            shared += block[:, at_shared:at_dt].astype(full)
            spot = (spots == own + j * heads) & (own < heads)
            steps += dot(block[:, at_dt : at_dt + LANES], spot.astype(low))
            small = stacks[layer][j, 0:16, :].astype(full)
            small = small[0:8, :] + small[8:16, :]
            kernel_out[layer, :, at : at + width] = small[0:CONV, :width]
            bias_out[layer : layer + 1, at : at + width] = small[CONV : CONV + 1, :width]
            smalls.append(small[:, width:])
        in_out[layer, :, 2 * INNER : INNER + XBC] = shared
        in_out[layer, :, INNER + XBC :] = steps[:, :HEADS]
        total = tree_sum(smalls)
        here = slice(layer, layer + 1)
        kernel_out[layer, :, INNER:] = total[0:CONV, : 2 * STATE]
        bias_out[here, INNER:] = total[CONV : CONV + 1, : 2 * STATE]
        at = 2 * STATE
        for row, ref in enumerate((shift_out, rate_out, skip_out)):
            ref[here, :] = total[row : row + 1, at : at + HEADS]
        at += LANES
        for ref in (gain_out, gate_out):
            size = ref.shape[1] // 8
            for row in range(8):
                ref[here, row * size : (row + 1) * size] = total[row : row + 1, at : at + size]
            at += size


def whole_spec(array):
    return pl.BlockSpec(array.shape, lambda *_: (0,) * len(array.shape))


def run(kernel, place, grid, inputs, in_specs, outputs, out_specs, scratch, duration=3, limit=56):
    out_specs = [
        whole_spec(item) if spec is None else spec for item, spec in zip(outputs, out_specs)
    ]
    in_specs = [whole_spec(item) if spec is None else spec for item, spec in zip(inputs, in_specs)]
    return pl.pallas_call(
        kernel,
        out_shape=outputs,
        grid_spec=pltpu.PrefetchScalarGridSpec(
            num_scalar_prefetch=1,
            grid=grid,
            in_specs=in_specs,
            out_specs=out_specs,
            scratch_shapes=scratch,
        ),
        compiler_params=pltpu.CompilerParams(vmem_limit_bytes=limit * 1024 * 1024),
        cost_estimate=pl.CostEstimate(
            flops=duration * 10**8, bytes_accessed=duration * 3 * 10**5, transcendentals=0
        ),
    )(place, *inputs)


def shape(*size, dtype=full):
    return jax.ShapeDtypeStruct(size, dtype)


def norm_rows(values, gain):
    scale = lax.rsqrt(jnp.mean(values * values, axis=-1, keepdims=True) + eps)
    return values * scale * gain


def per_device(
    hidden_in,
    segment_ids,
    norm_gain,
    in_weight,
    conv_weight,
    conv_bias,
    dt_bias,
    a_log,
    skip_weight,
    gate_norm,
    out_weight,
    cotangent,
):
    pieces, parts = lax.axis_size("seq"), lax.axis_size("fsdp")
    piece, part = lax.axis_index("seq"), lax.axis_index("fsdp")
    place = jnp.stack([piece, part]).astype(jnp.int32)
    tokens = hidden_in.shape[1]
    length = tokens * pieces
    heads = HEADS // pieces
    width = heads * HEADDIM
    mixed = width + 2 * STATE
    across = 2 * width + 2 * STATE + LANES
    rows_f = D // parts
    rows_out = D // (pieces * parts)
    core = piece % 2
    half = INNER // 2

    def columns(array, start, size):
        return lax.dynamic_slice_in_dim(array, start, size, array.ndim - 1)

    def own_xbc(array):
        return jnp.concatenate([columns(array, piece * width, width), array[..., INNER:]], axis=-1)

    def pad_lanes(array):
        return jnp.pad(array, [(0, 0)] * (array.ndim - 1) + [(0, LANES - array.shape[-1])])

    in_turned = jnp.swapaxes(in_weight, 1, 2)

    def own_in(layer, place):
        view = lambda size, at: pl.BlockSpec((1, size, rows_f), lambda _, where: (layer, at(where), 0))
        return run(
            functools.partial(pack_kernel, pieces),
            place,
            (1,),
            [in_turned] * 4,
            [
                view(width, lambda where: where[0]),
                view(width, lambda where: where[0] + pieces),
                view(2 * STATE, lambda where: INNER // STATE),
                view(HEADS, lambda where: (INNER + XBC) // HEADS),
            ],
            [shape(2 * width + 2 * STATE + DT_ROWS, rows_f, dtype=low)],
            [None],
            [],
        )[0]

    segment = segment_ids[0]
    places = jnp.arange(length)
    flags = []
    for tap in range(CONV - 1):
        back = CONV - 1 - tap
        flags.append((segment == jnp.roll(segment, back)) & (places >= back))
    for tap in range(CONV - 1):
        back = CONV - 1 - tap
        flags.append((segment == jnp.roll(segment, -back)) & (places < length - back))
    by_piece = segment.reshape(pieces, tokens)
    before = jnp.concatenate([jnp.full((1,), -1, jnp.int32), by_piece[:-1, -1]])[:, None]
    flags.append((by_piece == before).reshape(length))
    flags.append((by_piece == by_piece[:, -1:]).reshape(length))
    flags.append(jnp.broadcast_to(by_piece[:, -1:] == before, by_piece.shape).reshape(length))
    meta = jnp.stack([flag.astype(full) for flag in flags] + [segment.astype(full)], axis=1)
    meta = jnp.pad(meta, ((0, 0), (0, 16 - meta.shape[1])))
    segment_rows = segment.astype(full).reshape(pieces, 1, tokens)

    by_chunk = lambda size, back=False: pl.BlockSpec(
        (tokens, size), (lambda i, _: (pieces - 1 - i, 0)) if back else (lambda i, _: (i, 0))
    )

    normed = norm_rows(hidden_in[0], norm_gain[0]).astype(low)
    def whole_rows(rows):
        return lax.all_gather(rows, "fsdp", axis=0, tiled=True)

    own = own_in(0, place)
    following = own_in(1, after(place, own))
    place = after(place, following)
    if rows_f % LANES == 0:
        weights_in = [gather(own, "fsdp"), [whole_rows(following)]]
    else:
        weights_in = [[lax.all_gather(item, "fsdp", axis=1, tiled=True)] for item in (own, following)]
    out_mine = [whole_rows(columns(out_weight[0], after(core, own) * half, half))]
    later = after(core, *weights_in[0])
    out_mine.append(whole_rows(columns(out_weight[1], later * half, half)))
    weights_out = []

    def layer_params(layer):
        own = lambda array: columns(array[layer], piece * heads, heads)
        conv = jnp.concatenate([conv_weight[layer], conv_bias[layer][None]], axis=0)
        conv = jnp.pad(own_xbc(conv), ((0, 3), (0, 0)))
        head = jnp.pad(pad_lanes(jnp.stack([own(dt_bias), own(a_log)])), ((0, 6), (0, 0)))
        skip = jnp.repeat(own(skip_weight), HEADDIM)[None]
        return conv, head, skip

    hidden = hidden_in[0]
    stored = []
    for layer in range(LAYERS):
        hidden_before = hidden
        conv, head, skip = layer_params(layer)
        blocks = gather_seq(normed)
        inputs = [*blocks, *weights_in[layer], meta, segment_rows, conv, head, skip]
        in_specs = [None] * len(inputs)
        in_specs[-5] = by_chunk(16)
        in_specs[-4] = pl.BlockSpec((1, 1, tokens), lambda i, _: (i, 0, 0))
        result = run(
            functools.partial(forward_kernel, pieces, len(weights_in[layer])),
            place,
            (pieces,),
            inputs,
            in_specs,
            [shape(tokens, width, dtype=low)] * pieces
            + [
                shape(length, width, dtype=low),
                shape(length, D, dtype=low),
                shape(length, across),
                shape(length, mixed),
                shape(length, width),
                shape(pieces * width, STATE),
            ],
            [None] * pieces
            + [
                by_chunk(width),
                by_chunk(D),
                by_chunk(across),
                by_chunk(mixed),
                by_chunk(width),
                pl.BlockSpec((width, STATE), lambda i, _: (i, 0)),
            ],
            [
                pltpu.VMEM((width, STATE), full),
                pltpu.VMEM((tokens + 8, mixed), full),
                pltpu.VMEM((tokens, D), low),
                pltpu.VMEM((across, D), low),
            ],
            duration=16,
        )
        sends, (acted, normed_all, projected, pre, out, states) = result[:pieces], result[pieces:]
        mine = after(out_mine[layer], acted)
        weights_out.append(([mine], [swap(mine, "seq", 1)]))
        received = exchange(sends, "seq")
        mine, other = weights_out[layer]
        following = norm_gain[min(layer + 1, LAYERS - 1)][None]
        inputs = [*received, *mine, *other, gate_norm[layer][None], hidden, following]
        top = layer == LAYERS - 1
        grads_shape = [shape(tokens, width, dtype=low)] * pieces + [
            shape(tokens, D, dtype=low),
            shape(1, INNER),
        ]
        outputs = [shape(tokens, D), shape(tokens, D, dtype=low), shape(tokens, INNER, dtype=low)]
        if top:
            inputs.append(cotangent[0])
            outputs += grads_shape
        hidden, normed, acted_rows, *top_grads = run(
            functools.partial(
                rows_top_kernel if top else rows_forward_kernel, pieces, len(mine)
            ),
            place,
            (1,),
            inputs,
            [None] * len(inputs),
            outputs,
            [None] * len(outputs),
            [
                pltpu.VMEM((tokens, INNER), full),
            ],
        )
        stored.append(
            (
                hidden_before,
                (meta, segment_rows, conv, head, skip),
                (normed_all, projected, pre, out, states),
                acted,
                acted_rows,
            )
        )

    def weight_parts(layer, normed_all, grad_projected, branch_all, acted):
        own_gain = columns(gate_norm[layer], piece * width, width)[None]
        if rows_out % 16 == 0:
            return run(
                weight_kernel,
                place,
                (1,),
                [normed_all, grad_projected, branch_all, acted, own_gain],
                [None] * 5,
                [shape(parts, pieces, rows_out, across + width, dtype=low)],
                [None],
                [pltpu.VMEM((D, across + width), full)],
                duration=8,
            )[0]
        part_in = dot_tokens(normed_all, grad_projected)
        part_out = dot_tokens(branch_all, acted) * own_gain
        both = jnp.concatenate([part_in, part_out], axis=1).astype(low)
        return both.reshape(pieces, parts, rows_out, -1).swapaxes(0, 1)

    def weight_in_part(normed_all, grad_projected):
        return run(
            weight_in_kernel,
            place,
            (1,),
            [normed_all, grad_projected],
            [None] * 2,
            [shape(pieces, rows_out, across, dtype=low)] * parts,
            [None] * parts,
            [pltpu.VMEM((D, across), full)],
            duration=6,
        )

    def weight_out_part(branch_all, acted, small):
        own_gain = columns(gate_norm[0], piece * width, width)[None]
        return run(
            weight_out_kernel,
            place,
            (1,),
            [branch_all, acted, own_gain, small],
            [None] * 4,
            [shape(pieces + 2, rows_out, width, dtype=low)] * parts,
            [None] * parts,
            [pltpu.VMEM((D, width), full)],
        )

    def add_parts(blocks):
        return run(
            add_kernel,
            place,
            (1,),
            blocks,
            [None] * len(blocks),
            [shape(pieces, 16 + rows_out, block_lanes, dtype=low)],
            [None],
            [],
        )[0]

    small_lanes = mixed + LANES + (D + INNER) // 8
    block_lanes = max(across + width, small_lanes)
    apart = rows_out * width == small_lanes * 8

    def sum_pieces(partial, others):
        keep, give = partial
        taken = swap(give, "seq", 1)
        chips, chip, pair = pieces // 2, piece // 2, 2 * tokens

        def paired(which):
            cut = lambda array: lax.dynamic_slice_in_dim(array, which * pair, pair, 0)
            return cut(keep) + cut(taken).astype(full)

        total = after(paired(chip), *others)
        for mask in range(1, chips):
            total = total + swap(paired(chip ^ mask).astype(low), "seq", 2 * mask).astype(full)
        ours = lax.dynamic_slice_in_dim(total, core * tokens, tokens, 0)
        theirs = lax.dynamic_slice_in_dim(total, (1 - core) * tokens, tokens, 0)
        arrived = swap(theirs.astype(low), "seq", 1).astype(full)
        return jnp.where(
            core == 0,
            jnp.concatenate([ours, arrived], axis=1),
            jnp.concatenate([arrived, ours], axis=1),
        )

    grad_hidden = cotangent[0]
    grads_weight = [None] * LAYERS
    for layer in reversed(range(LAYERS)):
        hidden_before, shared, kept, acted, acted_rows = stored[layer]
        mine, other = weights_out[layer]
        inputs = [*mine, *other, gate_norm[layer][None], grad_hidden, acted_rows]
        result = top_grads
        if layer < LAYERS - 1:
            result = run(
                functools.partial(rows_backward_kernel, pieces, len(mine)),
                place,
                (1,),
                inputs,
                [None] * len(inputs),
                grads_shape,
                [None] * len(grads_shape),
                [pltpu.VMEM((tokens, INNER), full)],
            )
        sends, (branch, grad_gate_gain) = result[:pieces], result[pieces:]
        received = exchange(sends, "seq")
        if layer < LAYERS - 1:
            added = add_parts([shares, *smalls])
            grads_weight[layer + 1] = lax.all_to_all(added, "seq", 0, 0, tiled=True)
            received[0] = after(received[0], added)
        branch, *received = lax.optimization_barrier((branch, *received))
        branch_all = lax.all_gather(branch, "seq", axis=0, tiled=True)
        inputs = [*received, *weights_in[layer], *shared, norm_gain[layer][None], grad_gate_gain, *kept]
        in_specs = [None] * len(inputs)
        in_specs[-12] = by_chunk(16, True)
        in_specs[-11] = pl.BlockSpec((1, 1, tokens), lambda i, _: (pieces - 1 - i, 0, 0))
        in_specs[-5:-1] = [by_chunk(item.shape[1], True) for item in kept[:-1]]
        in_specs[-1] = pl.BlockSpec((width, STATE), lambda i, _: (pieces - 1 - i, 0))
        grad_projected, *partial, small = run(
            functools.partial(backward_kernel, pieces, len(weights_in[layer])),
            place,
            (pieces,),
            inputs,
            in_specs,
            [
                shape(length, across, dtype=low),
                shape(length, D // 2),
                shape(length, D // 2, dtype=low),
                shape(8, mixed + LANES + (D + INNER) // 8),
            ],
            [
                by_chunk(across, True),
                by_chunk(D // 2, True),
                by_chunk(D // 2, True),
                None,
            ],
            [
                pltpu.VMEM((width, STATE), full),
                pltpu.VMEM((tokens + 8, mixed), full),
                pltpu.VMEM((tokens, width), full),
                pltpu.VMEM((across, D), low),
                pltpu.VMEM((tokens, D), full),
                pltpu.VMEM((8, mixed), full),
                pltpu.VMEM((8, LANES), full),
                pltpu.VMEM((1, D), full),
            ],
            duration=29,
        )
        if layer == 0 and apart:
            weights = weight_in_part(kept[0], grad_projected)
            tails = weight_out_part(branch_all, acted, small)
            shares = exchange(weights, "fsdp")
            tails = exchange(tails, "fsdp")
            partial[1] = after(partial[1], *weights)
            grad_normed = sum_pieces(partial, tails)
        else:
            smalls = gather(small, "fsdp")
            grad_projected = after(grad_projected, *smalls)
            weights = weight_parts(layer, kept[0], grad_projected, branch_all, acted)
            shares = lax.all_to_all(weights, "fsdp", 0, 0, tiled=True)
            if layer < LAYERS - 1:
                partial[1] = after(partial[1], weights, grads_weight[layer + 1])
            grad_normed = sum_pieces(partial, [weights, *smalls])
        scaled = grad_normed * norm_gain[layer][None]
        scale = lax.rsqrt(jnp.mean(hidden_before * hidden_before, axis=-1, keepdims=True) + eps)
        unit = hidden_before * scale
        grad_hidden = grad_hidden + scale * (
            scaled - unit * jnp.mean(unit * scaled, axis=-1, keepdims=True)
        )

    blocks = [*shares, *tails] if apart else [shares, *smalls]
    blocks[0] = after(blocks[0], grad_normed, grads_weight[1])
    added = add_parts(blocks)
    grads_weight[0] = lax.all_to_all(added, "seq", 0, 0, tiled=True)
    grads = run(
        functools.partial(finish_kernel, pieces),
        place,
        (1,),
        grads_weight,
        [None] * LAYERS,
        [
            shape(LAYERS, D),
            shape(LAYERS, rows_out, PROJ),
            shape(LAYERS, CONV, XBC),
            shape(LAYERS, XBC),
            shape(LAYERS, HEADS),
            shape(LAYERS, HEADS),
            shape(LAYERS, HEADS),
            shape(LAYERS, INNER),
            shape(LAYERS, rows_out, INNER),
        ],
        [None] * 9,
        [],
    )
    return (hidden[None], grad_hidden[None], *grads)


def solution(mesh):
    in_specs = (
        P("fsdp", "seq", None),
        P("fsdp", None),
        P(),
        P(None, "fsdp", None),
        P(),
        P(),
        P(),
        P(),
        P(),
        P(),
        P(None, "fsdp", None),
        P("fsdp", "seq", None),
    )
    out_specs = (
        P("fsdp", "seq", None),
        P("fsdp", "seq", None),
        P(),
        P(None, ("seq", "fsdp"), None),
        P(),
        P(),
        P(),
        P(),
        P(),
        P(),
        P(None, ("seq", "fsdp"), None),
    )
    return jax.shard_map(
        per_device, mesh=mesh, in_specs=in_specs, out_specs=out_specs, check_vma=False
    )
```
